128 devices in a mesh: dp: 32 (over y, z, x_lo), tensor: 4 (over x_hi, core).
Axes of the slice: x: 4 (x_hi: 2, x_lo: 2; x = x_hi * 2 + x_lo), y: 4, z: 4, core: 2. Of those that a mesh axis runs over, the one named last changes fastest.
Arguments:
- tokens: bfloat16 [12608, 768], P('dp'), may hold values from -6 to 6
- norm_gain: float32 [4, 768], replicated, may hold values from 0.5 to 1.5
- norm_bias: float32 [4, 768], replicated, may hold values from -1.5 to 1.5
- attn_in: bfloat16 [2, 3, 768, 768], P(None, None, None, 'tensor'), may hold values from -0.21875 to 0.21875
- attn_out: bfloat16 [2, 768, 768], P(None, 'tensor'), may hold values from -0.75 to 0.75
- mlp_in: bfloat16 [768, 3072], P(None, 'tensor'), may hold values from -0.21875 to 0.21875
- mlp_out: bfloat16 [3072, 768], P('tensor'), may hold values from -0.109375 to 0.109375
- expert_in: bfloat16 [4, 768, 3072], P(None, None, 'tensor'), may hold values from -0.21875 to 0.21875
- expert_out: bfloat16 [4, 3072, 768], P(None, 'tensor'), may hold values from -0.109375 to 0.109375
- routes: int32 [12608, 2], P('dp'), may hold values from 0 to 3, as said below
- slot_index: int32 [12608, 2], P('dp'), may hold values from 0 to 168, as said below
- gate_weights: float32 [12608, 2], P('dp'), may hold values from 0.2 to 0.8
- cotangent: bfloat16 [12608, 768], P('dp'), may hold values from -6 to 6
Outputs:
- output: float32 [12608, 768], P('dp')
- token_grad: float32 [12608, 768], P('dp')
- norm_gain_grad: float32 [4, 768], P(None, 'dp')
- norm_bias_grad: float32 [4, 768], P(None, 'dp')
- attn_in_grad: float32 [2, 3, 768, 768], P(None, None, 'dp', 'tensor')
- attn_out_grad: float32 [2, 768, 768], P(None, 'tensor', 'dp')
- mlp_in_grad: float32 [768, 3072], P('dp', 'tensor')
- mlp_out_grad: float32 [3072, 768], P('tensor', 'dp')
- expert_in_grad: float32 [4, 768, 3072], P(None, 'dp', 'tensor')
- expert_out_grad: float32 [4, 3072, 768], P(None, 'tensor', 'dp')
The draws below stay inside these ranges and needn't reach their ends.
Inputs may be any that keep to these rules, and one draw needn't show every extreme that they name: `routes`: each row names two different experts. `slot_index`: within each aligned block of 394 rows (the rows of one index of dp) and for each expert, the choices that name it, first choices of all rows in row order and then second choices in row order, take slots 0, 1, 2 and so on up to 167; all later ones take 168, which marks a dropped choice; in every block some expert has more than 168 choices.
All inputs are finite; a program needn't handle non-finite values.
Results may differ from the reference program's by a relative error of at most 0.025.
Values may be sent and summed in bfloat16 or wider, within the bound.
A program may use at most 128 MiB of HBM per device.

```python
import math
import jax
import jax.numpy as jnp
from jax import lax

D = 768
HEADS = 12
HEAD_DIM = 64
FF = 3072
SEQ = 197
EXPERTS = 4
IMG_DEV = 2
TOK_DEV = 394
CAPACITY = 168
TOKENS = 12608
N_DP = 32


def route_pair(key):
    first_pick = jax.random.randint(jax.random.fold_in(key, 11), (TOKENS,), 0, EXPERTS)
    offset = jax.random.randint(jax.random.fold_in(key, 12), (TOKENS,), 1, EXPERTS)
    second_pick = (first_pick + offset) % EXPERTS
    routes = jnp.stack([first_pick, second_pick], axis=1).astype(jnp.int32)
    blocks = TOKENS // TOK_DEV
    ordered = jnp.transpose(routes.reshape(blocks, TOK_DEV, 2), (0, 2, 1)).reshape(blocks, 2 * TOK_DEV)
    onehot = (ordered[:, :, None] == jnp.arange(EXPERTS, dtype=jnp.int32)[None, None, :]).astype(jnp.int32)
    counts = jnp.cumsum(onehot, axis=1) - onehot
    position = jnp.minimum(jnp.sum(counts * onehot, axis=2), CAPACITY)
    slot_table = jnp.transpose(position.reshape(blocks, 2, TOK_DEV), (0, 2, 1)).reshape(TOKENS, 2)
    return (routes, slot_table.astype(jnp.int32))


def draw_routes(key, part):
    return route_pair(key)[0]


def draw_slot_index(key, part):
    return route_pair(key)[1]


def spiked(entries, key, source, target, shards_of, factor):
    def block_of(dim):
        return (jnp.arange(entries.shape[dim]) // (entries.shape[dim] // shards_of)).reshape((-1,) + (1,) * (entries.ndim - 1 - dim))

    one_side = jax.random.permutation(key, shards_of)[block_of(target)]
    far = (block_of(target) + shards_of // 2) % shards_of
    return jnp.where((block_of(source) == one_side) | (block_of(source) == far), factor * entries, entries)


def shard_levels(key, shape, pieces, low, high):
    def one(dim, parts):
        steps = jax.random.uniform(jax.random.fold_in(jax.random.fold_in(key, 6), dim), (parts,), jnp.float32, low / len(pieces), high / len(pieces))
        return jnp.repeat(jnp.exp(steps), shape[dim] // parts).reshape((-1,) + (1,) * (len(shape) - dim - 1))

    factor_of = one(*pieces[0])
    for cut in pieces[1:]:
        factor_of = factor_of * one(*cut)
    return factor_of


def scatter_about(stream_key, dims, deviation, most, pieces=(), kind=jnp.bfloat16):
    result = jax.random.normal(stream_key, dims, jnp.float32) * deviation
    if len(pieces) > 0:
        result = shard_levels(stream_key, dims, pieces, -0.22, 0.18) * result
    return jnp.clip(result, min=-most, max=most).astype(kind)


def gaussian_with(rng, dims, deviation, reach, cuts, heavy, held_as=jnp.bfloat16):
    drawn = deviation * jax.random.normal(rng, dims, jnp.float32)
    if cuts:
        drawn = drawn * shard_levels(rng, dims, cuts, -0.22, 0.18)
    return jnp.clip(spiked(drawn, jax.random.fold_in(rng, 3), *heavy), -reach, reach).astype(held_as)


def setup_inputs(seed: int = 0) -> dict:
    arg_keys = jax.random.split(jax.random.key(seed), 14)
    tokens = scatter_about(arg_keys[0], (TOKENS, D), 1.0, 6.0, ((0, 32),))
    norm_gain = jnp.clip(1.0 + 0.1 * jax.random.normal(arg_keys[1], (4, D), jnp.float32), 0.5, 1.5)
    norm_bias = scatter_about(arg_keys[2], (4, D), 0.3, 1.5, (), jnp.float32)
    attn_in = scatter_about(arg_keys[3], (2, 3, D, D), D ** -0.5, 0.21875, ((3, 4),))
    attn_out = scatter_about(arg_keys[4], (2, D, D), HEAD_DIM ** -0.5, 0.75, ((1, 4),))
    mlp_in = scatter_about(arg_keys[5], (D, FF), D ** -0.5, 0.21875, ((1, 4),))
    mlp_out = scatter_about(arg_keys[6], (FF, D), FF ** -0.5, 0.109375, ((0, 4),))
    expert_in = scatter_about(arg_keys[7], (EXPERTS, D, FF), D ** -0.5, 0.21875, ((2, 4),))
    expert_out = scatter_about(arg_keys[8], (EXPERTS, FF, D), FF ** -0.5, 0.109375, ((1, 4),))
    routes = draw_routes(jax.random.fold_in(arg_keys[13], 71), 0)
    slot_index = draw_slot_index(jax.random.fold_in(arg_keys[13], 71), 0)
    gate_weights = jnp.clip(0.2 + 0.6 * jax.random.uniform(arg_keys[11], (TOKENS, 2), jnp.float32) ** shard_levels(arg_keys[11], (TOKENS, 2), ((0, 32),), -0.2, 0.2), 0.2, 0.8)
    cotangent = gaussian_with(arg_keys[12], (TOKENS, D), 1.0, 6.0, ((0, 32),), (0, 1, 32, 2.75))
    return {"tokens": tokens, "norm_gain": norm_gain, "norm_bias": norm_bias, "attn_in": attn_in, "attn_out": attn_out, "mlp_in": mlp_in, "mlp_out": mlp_out, "expert_in": expert_in, "expert_out": expert_out, "routes": routes, "slot_index": slot_index, "gate_weights": gate_weights, "cotangent": cotangent}


@jax.custom_vjp
def low(v):
    return lax.optimization_barrier(v.astype(jnp.bfloat16)).astype(jnp.float32)

@jax.custom_vjp
def low_back(v):
    return v

def low_keep(v):
    return (low(v), None)

def low_pass(kept, grad):
    return (grad,)

def back_keep(v):
    return (v, None)

def back_low(kept, grad):
    return (low(grad),)
low.defvjp(low_keep, low_pass)
low_back.defvjp(back_keep, back_low)
NORM_EPSILON = 1e-06
HIGHEST = lax.Precision.HIGHEST

def layer_norm(values, gain_row, bias_row):
    center = values - lax.optimization_barrier(jnp.mean(values, axis=-1, keepdims=True))
    spread = lax.optimization_barrier(jnp.mean(center * center, axis=-1, keepdims=True))
    return center * lax.rsqrt(spread + NORM_EPSILON) * gain_row + bias_row

def gelu_exact(values):
    return jax.nn.gelu(values, approximate=False)

def attend_group(triple):
    queries, keys_in, values_in = triple
    scaling = 1.0 / math.sqrt(HEAD_DIM)
    scores = low_back(jnp.einsum('bqhd,bkhd->bhqk', queries, keys_in, precision=HIGHEST) * scaling)
    weights = low(jax.nn.softmax(scores, axis=-1))
    return jnp.einsum('bhqk,bkhd->bqhd', weights, values_in, precision=HIGHEST)

def attention(normed, weight_in, weight_out):
    projected = low_back(low(jnp.einsum('nd,jde->jne', normed, weight_in, precision=HIGHEST)))
    shaped = projected.reshape(3, N_DP, IMG_DEV, SEQ, HEADS, HEAD_DIM)
    mixture = lax.map(jax.checkpoint(attend_group), (shaped[0], shaped[1], shaped[2]))
    mixture = low_back(low(mixture.reshape(TOKENS, D)))
    return low_back(jnp.dot(mixture, weight_out, precision=HIGHEST))

def feed_forward(normed, weight_in, weight_out):
    hidden = low_back(jnp.dot(normed, weight_in, precision=HIGHEST))
    active = low(gelu_exact(hidden))
    return low_back(jnp.dot(active, weight_out, precision=HIGHEST))

def experts(normed, weight_in, weight_out, routes, slot_index, gate_weights):
    row_count = normed.shape[0]
    owners = jnp.broadcast_to((jnp.arange(row_count, dtype=jnp.int32) // TOK_DEV)[:, None], routes.shape)
    buffer = jnp.zeros((N_DP, EXPERTS, CAPACITY + 1, D), jnp.float32)
    buffer = buffer.at[owners, routes, slot_index].add(jnp.broadcast_to(normed[:, None, :], (row_count, 2, D)))
    hidden = low_back(jnp.einsum('becd,edf->becf', buffer, weight_in, precision=HIGHEST))
    active = low(gelu_exact(hidden))
    expert_rows = low_back(jnp.einsum('becf,efd->becd', active, weight_out, precision=HIGHEST))
    picked = expert_rows[owners, routes, slot_index]
    weighting = gate_weights * (slot_index < CAPACITY).astype(jnp.float32)
    return lax.optimization_barrier(jnp.sum(picked * weighting[:, :, None], axis=1))

def forward(tokens, norm_gain, norm_bias, attn_in, attn_out, mlp_in, mlp_out, expert_in, expert_out, routes, slot_index, gate_weights):
    normed = low(layer_norm(tokens, norm_gain[0], norm_bias[0]))
    stream = tokens + attention(normed, attn_in[0], attn_out[0])
    normed = low(layer_norm(stream, norm_gain[1], norm_bias[1]))
    stream = stream + feed_forward(normed, mlp_in, mlp_out)
    normed = low(layer_norm(stream, norm_gain[2], norm_bias[2]))
    stream = stream + attention(normed, attn_in[1], attn_out[1])
    normed = low(layer_norm(stream, norm_gain[3], norm_bias[3]))
    return stream + experts(normed, expert_in, expert_out, routes, slot_index, gate_weights)

def reference(tokens, norm_gain, norm_bias, attn_in, attn_out, mlp_in, mlp_out, expert_in, expert_out, routes, slot_index, gate_weights, cotangent):
    floats = tuple((argument.astype(jnp.float32) for argument in (tokens, norm_gain, norm_bias, attn_in, attn_out, mlp_in, mlp_out, expert_in, expert_out)))
    gate_floats = gate_weights.astype(jnp.float32)

    def apply_layer(tokens_f, gain_f, bias_f, attn_in_f, attn_out_f, mlp_in_f, mlp_out_f, expert_in_f, expert_out_f):
        return forward(tokens_f, gain_f, bias_f, attn_in_f, attn_out_f, mlp_in_f, mlp_out_f, expert_in_f, expert_out_f, routes, slot_index, gate_floats)
    output, pullback = jax.vjp(apply_layer, *floats)
    gradients = pullback(cotangent.astype(jnp.float32))
    return (output, gradients[0], gradients[1], gradients[2], gradients[3], gradients[4], gradients[5], gradients[6], gradients[7], gradients[8])
```

```python
import functools
import math

import jax
import jax.numpy as jnp
from jax import lax
from jax.experimental import pallas as pl
from jax.experimental.pallas import tpu as pltpu
from jax.sharding import PartitionSpec as P

HEAD_DIM = 64
SEQ = 197
PAD = 208
CAPACITY = 168
NORM_EPSILON = 1e-06
MESH = pl.DeviceIdType.MESH
F32 = jnp.float32
BF16 = jnp.bfloat16


def tensor_sum_kernel(x_ref, o_ref, from_core, mine, from_chip, send, recv):
    dp = lax.axis_index("dp")
    t = lax.axis_index("tensor")
    core = lax.rem(t, 2)
    other = (dp, t + 1 - 2 * core)
    far = (dp, lax.rem(t + 2, 4))
    barrier = pltpu.get_barrier_semaphore()
    for device in (other, far):
        pl.semaphore_signal(barrier, inc=1, device_id=device, device_id_type=MESH)
    pl.semaphore_wait(barrier, 2)
    count = x_ref.shape[0] // 2

    def remote(source, target, slot, device):
        return pltpu.make_async_remote_copy(
            src_ref=source,
            dst_ref=target,
            send_sem=send.at[slot],
            recv_sem=recv.at[slot],
            device_id=device,
            device_id_type=MESH,
        )

    first = remote(x_ref.at[pl.ds((1 - core) * count, count)], from_core, 0, other)
    first.start()
    first.wait()
    for i in range(count):
        mine[i] = (x_ref[core * count + i].astype(F32) + from_core[i].astype(F32)).astype(BF16)
    second = remote(mine, from_chip, 1, far)
    second.start()
    second.wait()
    for i in range(count):
        o_ref[core * count + i] = mine[i].astype(F32) + from_chip[i].astype(F32)
    half = o_ref.at[pl.ds(core * count, count)]
    third = remote(half, half, 2, other)
    third.start()
    third.wait()


def tensor_sum(parts, collective_id):
    rows, width = parts[0].shape
    stacked = jnp.stack(
        [
            jnp.pad(p.astype(BF16)[i * SEQ : (i + 1) * SEQ], ((0, PAD - SEQ), (0, 0)))
            for i in range(2)
            for p in parts
        ]
    )
    count = len(parts)
    total = pl.pallas_call(
        tensor_sum_kernel,
        out_shape=jax.ShapeDtypeStruct(stacked.shape, F32),
        in_specs=[pl.BlockSpec(memory_space=pltpu.VMEM)],
        out_specs=pl.BlockSpec(memory_space=pltpu.VMEM),
        scratch_shapes=[
            pltpu.VMEM((count, PAD, width), BF16),
            pltpu.VMEM((count, PAD, width), BF16),
            pltpu.VMEM((count, PAD, width), BF16),
            pltpu.SemaphoreType.DMA((3,)),
            pltpu.SemaphoreType.DMA((3,)),
        ],
        compiler_params=pltpu.CompilerParams(
            collective_id=collective_id, has_side_effects=True, vmem_limit_bytes=40 << 20
        ),
        name="tensor_sum",
    )(stacked)
    return [
        jnp.concatenate([total[i, :SEQ], total[count + i, :SEQ]], axis=0) for i in range(count)
    ]


def grid_device(y, z, x):
    return (lax.rem(y + 8, 4) * 4 + lax.rem(z + 8, 4)) * 2 + x


def image_sum_kernel(orders, *refs):
    n = len(orders)
    g_refs, o_refs = refs[:n], refs[n : 2 * n]
    owns, gots, sums, gots2, totals, outs3, gots3 = (
        refs[2 * n + k * n : 2 * n + (k + 1) * n] for k in range(7)
    )
    send, recv, local_sem = refs[9 * n :]
    dp = lax.axis_index("dp")
    t = lax.axis_index("tensor")
    y, z, x = dp // 8, lax.rem(dp // 2, 4), lax.rem(dp, 2)

    barrier = pltpu.get_barrier_semaphore()
    for k in (1, 2, 3):
        for device in (grid_device(y + k, z, x), grid_device(y, z + k, x)):
            pl.semaphore_signal(barrier, inc=1, device_id=(device, t), device_id_type=MESH)
    pl.semaphore_signal(barrier, inc=1, device_id=(grid_device(y, z, 1 - x), t), device_id_type=MESH)
    pl.semaphore_wait(barrier, 7)

    def remote(source, target, slot, device):
        return pltpu.make_async_remote_copy(
            src_ref=source,
            dst_ref=target,
            send_sem=send.at[slot],
            recv_sem=recv.at[slot],
            device_id=(device, t),
            device_id_type=MESH,
        )

    first, locals_ = [], []
    for i, order in enumerate(orders):
        copies = []
        for k in (2, 1, 3):
            if order == "y":
                source, device = g_refs[i].at[:, lax.rem(y + k, 4)], grid_device(y + k, z, x)
            else:
                source, device = g_refs[i].at[:, :, lax.rem(z + k, 4)], grid_device(y, z + k, x)
            copies.append(remote(source, gots[i].at[k - 1], i * 7 + k - 1, device))
            copies[-1].start()
        first.append(copies)
        source = g_refs[i].at[:, y] if order == "y" else g_refs[i].at[:, :, z]
        locals_.append(pltpu.make_async_copy(source, owns[i], local_sem.at[i]))
        locals_[-1].start()
    second = []
    for i, order in enumerate(orders):
        locals_[i].wait()
        for copy in first[i]:
            copy.wait()

        def add(m, carry, i=i):
            for b in range(4):
                acc = owns[i][m, b].astype(F32)
                for k in range(3):
                    acc = acc + gots[i][k, m, b].astype(F32)
                sums[i][m, b] = acc.astype(BF16)
            return carry

        lax.fori_loop(0, owns[i].shape[0], add, 0)
        copies = []
        for k in (2, 1, 3):
            if order == "y":
                index, device = lax.rem(z + k, 4), grid_device(y, z + k, x)
            else:
                index, device = lax.rem(y + k, 4), grid_device(y + k, z, x)
            copies.append(remote(sums[i].at[:, index], gots2[i].at[k - 1], i * 7 + 2 + k, device))
            copies[-1].start()
        second.append(copies)
    third = []
    for i, order in enumerate(orders):
        for copy in second[i]:
            copy.wait()
        own = z if order == "y" else y

        def add(m, carry, i=i, own=own):
            acc = sums[i][m, own].astype(F32)
            for k in range(3):
                acc = acc + gots2[i][k, m].astype(F32)
            totals[i][m] = acc
            return carry

        count = owns[i].shape[0]
        lax.fori_loop(0, count, add, 0)
        other = pl.ds(pl.multiple_of((1 - x) * 24, 8), 24)
        if count > 1:
            for m in range(0, count, 2):
                pair = jnp.concatenate([totals[i][m, other], totals[i][m + 1, other]], axis=0)
                outs3[i][m // 2] = pair.astype(BF16)
        else:
            alone = totals[i][0, other]
            outs3[i][0] = jnp.concatenate([alone, alone], axis=0).astype(BF16)
        third.append(remote(outs3[i], gots3[i], i * 7 + 6, grid_device(y, z, 1 - x)))
        third[-1].start()
    for i in range(n):
        third[i].wait()
        mine = pl.ds(pl.multiple_of(x * 24, 8), 24)
        for m in range(owns[i].shape[0]):
            theirs = gots3[i][m // 2].astype(F32)
            o_refs[i][m] = totals[i][m, mine] + theirs[24 * (m % 2) : 24 * (m % 2) + 24]


def image_sum(groups, orders, collective_id):
    n = len(groups)
    shaped = [g.reshape(g.shape[0], 4, 4, 48, g.shape[2]) for g in groups]
    dims = [(g.shape[0], g.shape[2]) for g in groups]
    scratch = (
        [pltpu.VMEM((c, 4, 48, w), BF16) for c, w in dims]
        + [pltpu.VMEM((3, c, 4, 48, w), BF16) for c, w in dims]
        + [pltpu.VMEM((c, 4, 48, w), BF16) for c, w in dims]
        + [pltpu.VMEM((3, c, 48, w), BF16) for c, w in dims]
        + [pltpu.VMEM((c, 48, w), F32) for c, w in dims]
        + [pltpu.VMEM(((c + 1) // 2, 48, w), BF16) for c, w in dims]
        + [pltpu.VMEM(((c + 1) // 2, 48, w), BF16) for c, w in dims]
        + [
            pltpu.SemaphoreType.DMA((7 * n,)),
            pltpu.SemaphoreType.DMA((7 * n,)),
            pltpu.SemaphoreType.DMA((n,)),
        ]
    )
    return pl.pallas_call(
        functools.partial(image_sum_kernel, orders),
        out_shape=[jax.ShapeDtypeStruct((c, 24, w), F32) for c, w in dims],
        in_specs=[pl.BlockSpec(memory_space=pl.ANY)] * n,
        out_specs=[pl.BlockSpec(memory_space=pltpu.VMEM)] * n,
        scratch_shapes=scratch,
        compiler_params=pltpu.CompilerParams(
            collective_id=collective_id, has_side_effects=True, vmem_limit_bytes=50 << 20
        ),
        name="image_sum",
    )(*shaped)


def layer_norm(values, gain_row, bias_row):
    center = values - jnp.mean(values, axis=-1, keepdims=True)
    spread = jnp.mean(center * center, axis=-1, keepdims=True)
    return center * lax.rsqrt(spread + NORM_EPSILON) * gain_row + bias_row


def norm_backward(values, gain_row, bias_row, upstream):
    unused, pullback = jax.vjp(layer_norm, values, gain_row, bias_row)
    return pullback(upstream)


def gelu_exact(values):
    return jax.nn.gelu(values, approximate=False)


def gelu_back(hidden, upstream):
    unused, pullback = jax.vjp(gelu_exact, hidden)
    return pullback(upstream)[0]


def head_scores(shaped):
    scaling = 1.0 / math.sqrt(HEAD_DIM)
    return jnp.einsum("bqhd,bkhd->bhqk", shaped[0], shaped[1], preferred_element_type=F32) * scaling


def head_forward(normed, weight_in, weight_out):
    projected = jnp.einsum("nd,jde->jne", normed, weight_in, preferred_element_type=F32).astype(BF16)
    images = normed.shape[0] // SEQ
    local_heads = weight_in.shape[2] // HEAD_DIM
    shaped = projected.reshape(3, images, SEQ, local_heads, HEAD_DIM)
    scores = head_scores(shaped)
    highest = jnp.max(scores, axis=-1, keepdims=True)
    log_total = highest + jnp.log(jnp.sum(jnp.exp(scores - highest), axis=-1, keepdims=True))
    weights = jnp.exp(scores - log_total).astype(BF16)
    mixture = jnp.einsum("bhqk,bkhd->bqhd", weights, shaped[2], preferred_element_type=F32)
    mixture = mixture.astype(BF16).reshape(normed.shape[0], weight_in.shape[2])
    partial_sum = jnp.dot(mixture, weight_out, preferred_element_type=F32)
    return (partial_sum, (shaped, log_total, mixture))


def head_backward(normed, weight_in, weight_out, stored, upstream):
    shaped, log_total, mixture = stored
    scaling = 1.0 / math.sqrt(HEAD_DIM)
    upstream_low = upstream.astype(BF16)
    grad_out = jnp.einsum("nd,ne->de", upstream_low, mixture, preferred_element_type=F32)
    d_mixture = jnp.einsum("nd,ed->ne", upstream_low, weight_out, preferred_element_type=F32).astype(BF16)
    d_mixture = d_mixture.reshape(shaped.shape[1:])
    probability = jnp.exp(head_scores(shaped) - log_total)
    d_weights = jnp.einsum("bqhd,bkhd->bhqk", d_mixture, shaped[2], preferred_element_type=F32)
    centered = d_weights - jnp.sum(probability * d_weights, axis=-1, keepdims=True)
    d_scores = (probability * centered).astype(BF16)
    d_query = (
        jnp.einsum("bhqk,bkhd->bqhd", d_scores, shaped[1], preferred_element_type=F32) * scaling
    ).astype(BF16)
    d_keys = (
        jnp.einsum("bhqk,bqhd->bkhd", d_scores, shaped[0], preferred_element_type=F32) * scaling
    ).astype(BF16)
    d_values = jnp.einsum(
        "bhqk,bqhd->bkhd", probability.astype(BF16), d_mixture, preferred_element_type=F32
    ).astype(BF16)
    flat = [v.reshape(normed.shape[0], weight_in.shape[2]) for v in (d_query, d_keys, d_values)]
    d_projected = jnp.concatenate(flat, axis=1)
    grad_in = jnp.einsum("nd,ne->de", normed, d_projected, preferred_element_type=F32)
    d_normed = jnp.einsum("jne,jde->nd", jnp.stack(flat), weight_in, preferred_element_type=F32)
    grads = jnp.concatenate([grad_in.astype(BF16), grad_out.astype(BF16)], axis=1)
    return (d_normed, grads)


def dense_forward(normed, weight_in, weight_out):
    hidden = jnp.dot(normed, weight_in, preferred_element_type=F32)
    active = gelu_exact(hidden).astype(BF16)
    return (jnp.dot(active, weight_out, preferred_element_type=F32), (hidden, active))


def dense_backward(normed, weight_in, weight_out, stored, upstream):
    hidden, active = stored
    upstream_low = upstream.astype(BF16)
    grad_out = jnp.einsum("nd,nf->df", upstream_low, active, preferred_element_type=F32)
    d_active = jnp.einsum("nd,fd->nf", upstream_low, weight_out, preferred_element_type=F32)
    d_hidden = gelu_back(hidden, d_active).astype(BF16)
    grad_in = jnp.einsum("nd,nf->df", normed, d_hidden, preferred_element_type=F32)
    d_normed = jnp.einsum("nf,df->nd", d_hidden, weight_in, preferred_element_type=F32)
    return (d_normed, grad_in.astype(BF16), grad_out.astype(BF16))


def experts(normed, weight_in, weight_out, routes, slot_index, gate_weights, cotangent):
    count = weight_in.shape[0]
    width = normed.shape[1]
    flat = jnp.where(slot_index < CAPACITY, routes * CAPACITY + slot_index, -1)
    slots = lax.broadcasted_iota(jnp.int32, (count * CAPACITY, normed.shape[0]), 0)
    hits = [slots == flat[:, k][None, :] for k in range(2)]
    pick = jnp.logical_or(*hits).astype(BF16)
    gate = sum(
        jnp.sum(jnp.where(hits[k], gate_weights[:, k][None, :], 0.0), axis=1, keepdims=True)
        for k in range(2)
    )
    shape = (count, CAPACITY, width)
    buffer = jnp.dot(pick, normed, preferred_element_type=F32).astype(BF16).reshape(shape)
    d_rows = jnp.dot(pick, cotangent, preferred_element_type=F32) * gate
    d_rows = d_rows.astype(BF16).reshape(shape)
    hidden = jnp.einsum("ecd,edf->ecf", buffer, weight_in, preferred_element_type=F32)
    active = gelu_exact(hidden).astype(BF16)
    rows = jnp.einsum("ecf,efd->ecd", active, weight_out, preferred_element_type=F32)
    weighted = (rows.reshape(-1, width) * gate).astype(BF16)
    forward = jnp.einsum("sn,sd->nd", pick, weighted, preferred_element_type=F32)
    grad_out = jnp.einsum("ecd,ecf->edf", d_rows, active, preferred_element_type=F32)
    d_active = jnp.einsum("ecd,efd->ecf", d_rows, weight_out, preferred_element_type=F32)
    d_hidden = gelu_back(hidden, d_active).astype(BF16)
    grad_in = jnp.einsum("ecd,ecf->edf", buffer, d_hidden, preferred_element_type=F32)
    d_buffer = jnp.einsum("ecf,edf->ecd", d_hidden, weight_in, preferred_element_type=F32)
    d_normed = jnp.einsum(
        "sn,sd->nd", pick, d_buffer.reshape(-1, width).astype(BF16), preferred_element_type=F32
    )
    return (forward, d_normed, grad_in.astype(BF16), grad_out.astype(BF16))


def local(
    tokens,
    norm_gain,
    norm_bias,
    attn_in,
    attn_out,
    mlp_in,
    mlp_out,
    expert_in,
    expert_out,
    routes,
    slot_index,
    gate_weights,
    cotangent,
):
    stream_a = tokens.astype(F32)
    normed_a = layer_norm(stream_a, norm_gain[0], norm_bias[0]).astype(BF16)
    part, stored_a = head_forward(normed_a, attn_in[0], attn_out[0])
    stream_b = stream_a + tensor_sum([part], 1)[0]
    normed_b = layer_norm(stream_b, norm_gain[1], norm_bias[1]).astype(BF16)
    part, stored_b = dense_forward(normed_b, mlp_in, mlp_out)
    stream_c = stream_b + tensor_sum([part], 1)[0]
    normed_c = layer_norm(stream_c, norm_gain[2], norm_bias[2]).astype(BF16)
    part, stored_c = head_forward(normed_c, attn_in[1], attn_out[1])
    stream_d = stream_c + tensor_sum([part], 1)[0]
    normed_d = layer_norm(stream_d, norm_gain[3], norm_bias[3]).astype(BF16)
    part, d_part, grad_ein, grad_eout = experts(
        normed_d, expert_in, expert_out, routes, slot_index, gate_weights, cotangent
    )
    mixed_d, d_normed = tensor_sum([part, d_part], 2)
    output = stream_d + mixed_d
    upstream = cotangent.astype(F32)
    d_stream, gain_d, bias_d = norm_backward(stream_d, norm_gain[3], norm_bias[3], d_normed)
    upstream = upstream + d_stream
    d_part, grads_c = head_backward(normed_c, attn_in[1], attn_out[1], stored_c, upstream)
    d_normed = tensor_sum([d_part], 1)[0]
    d_stream, gain_c, bias_c = norm_backward(stream_c, norm_gain[2], norm_bias[2], d_normed)
    upstream = upstream + d_stream
    d_part, grad_min, grad_mout = dense_backward(normed_b, mlp_in, mlp_out, stored_b, upstream)
    d_normed = tensor_sum([d_part], 1)[0]
    d_stream, gain_b, bias_b = norm_backward(stream_b, norm_gain[1], norm_bias[1], d_normed)
    upstream = upstream + d_stream
    d_part, grads_a = head_backward(normed_a, attn_in[0], attn_out[0], stored_a, upstream)
    d_normed = tensor_sum([d_part], 1)[0]
    d_stream, gain_a, bias_a = norm_backward(stream_a, norm_gain[0], norm_bias[0], d_normed)
    token_grad = upstream + d_stream
    norms = jnp.stack([gain_a, gain_b, gain_c, gain_d, bias_a, bias_b, bias_c, bias_d], axis=1)
    norms = jnp.pad(norms, ((0, 0), (0, 120))).astype(BF16)[None]
    ein, eout, dense, heads, norms = image_sum(
        [
            grad_ein,
            grad_eout,
            jnp.stack([grad_min, grad_mout]),
            jnp.stack([grads_a, grads_c]),
            norms,
        ],
        ("y", "z", "y", "z", "y"),
        3,
    )
    head_width = attn_out.shape[1]
    attn_in_sum = jnp.stack(
        [heads[:, :, c * head_width : (c + 1) * head_width] for c in range(3)], axis=1
    )
    return (
        output,
        token_grad,
        norms[0, :, :4].T,
        norms[0, :, 4:8].T,
        attn_in_sum,
        jnp.swapaxes(heads[:, :, 3 * head_width :], 1, 2),
        dense[0],
        dense[1].T,
        ein,
        jnp.swapaxes(eout, 1, 2),
    )


def solution(mesh):
    placed = (
        P("dp", None),
        P(),
        P(),
        P(None, None, None, "tensor"),
        P(None, "tensor", None),
        P(None, "tensor"),
        P("tensor", None),
        P(None, None, "tensor"),
        P(None, "tensor", None),
        P("dp", None),
        P("dp", None),
        P("dp", None),
        P("dp", None),
    )
    return jax.shard_map(
        local,
        mesh=mesh,
        in_specs=placed,
        out_specs=(
            P("dp", None),
            P("dp", None),
            P(None, "dp"),
            P(None, "dp"),
            P(None, None, "dp", "tensor"),
            P(None, "tensor", "dp"),
            P("dp", "tensor"),
            P("tensor", "dp"),
            P(None, "dp", "tensor"),
            P(None, "tensor", "dp"),
        ),
        check_vma=False,
    )
```

```python
import functools

import jax
import jax.numpy as jnp
from jax import lax
from jax.experimental import pallas as pl
from jax.experimental.pallas import tpu as pltpu
from jax.sharding import PartitionSpec as P

D = 768
HEAD_DIM = 64
SEQ = 197
HALF = 112
PAD = 2 * HALF
CAPACITY = 168
SLOTS = 176
EXPERTS = 4
NORM_EPSILON = 1e-06
MESH = pl.DeviceIdType.MESH
F32 = jnp.float32
BF16 = jnp.bfloat16


def dot(a, b):
    return lax.dot_general(a, b, (((1,), (0,)), ((), ())), preferred_element_type=F32)


def dot_nt(a, b):
    return lax.dot_general(a, b, (((1,), (1,)), ((), ())), preferred_element_type=F32)


def dot_tn(a, b):
    return lax.dot_general(a, b, (((0,), (0,)), ((), ())), preferred_element_type=F32)


def grid_device(y, z, x):
    return (lax.rem(y + 8, 4) * 4 + lax.rem(z + 8, 4)) * 2 + x


def normalize(v):
    center = v - jnp.mean(v, axis=-1, keepdims=True)
    spread = jnp.mean(center * center, axis=-1, keepdims=True)
    scale = lax.rsqrt(spread + NORM_EPSILON)
    return center * scale, scale


def norm_back(v, gain_row, upstream):
    nhat, scale = normalize(v)
    scaled = upstream * gain_row
    mean = jnp.mean(scaled, axis=-1, keepdims=True)
    along = jnp.mean(scaled * nhat, axis=-1, keepdims=True)
    dv = (scaled - mean - nhat * along) * scale
    gain_term = jnp.sum(upstream * nhat, axis=0, keepdims=True)
    bias_term = jnp.sum(upstream, axis=0, keepdims=True)
    return dv, gain_term, bias_term


def gelu_pair(h):
    phi = 0.5 * (1.0 + lax.erf(h * 0.7071067811865476))
    density = jnp.exp(-0.5 * h * h) * 0.3989422804014327
    return (h * phi).astype(BF16), phi + h * density


def head_mask(h, width):
    lane = lax.broadcasted_iota(jnp.int32, (1, width), 1)
    return jnp.logical_and(lane >= h * HEAD_DIM, lane < (h + 1) * HEAD_DIM)


def only(h, v):
    return jnp.where(head_mask(h, v.shape[1]), v, jnp.zeros((), v.dtype))


class TensorLinks:
    def __init__(self, refs, sems):
        self.full, self.pair_out, self.pair_in, self.far_out, self.far_in = refs
        self.sems = sems
        self.dp = lax.axis_index("dp")
        t = lax.axis_index("tensor")
        self.core = lax.rem(t, 2)
        self.other = t + 1 - 2 * self.core
        self.far = lax.rem(t + 2, 4)
        self.pairs, self.fars, self.gathers = {}, {}, {}

    def copy(self, source, target, slot, device):
        send, recv = self.sems
        c = pltpu.make_async_remote_copy(
            src_ref=source,
            dst_ref=target,
            send_sem=send.at[slot],
            recv_sem=recv.at[slot],
            device_id=(self.dp, device),
            device_id_type=MESH,
        )
        c.start()
        return c

    def share(self, ch, value):
        self.full[ch, 0] = value[:HALF]
        self.full[ch, 1] = value[HALF:]
        self.pair_out[ch] = self.full[ch, 1 - self.core].astype(BF16)
        self.pairs[ch] = self.copy(self.pair_out.at[ch], self.pair_in.at[ch], ch, self.other)

    def swap(self, ch, parity):
        self.pairs.pop(ch).wait()
        mine = self.full[ch, self.core] + self.pair_in[ch].astype(F32)
        self.far_out[ch] = mine.astype(BF16)
        self.fars[ch] = self.copy(
            self.far_out.at[ch], self.far_in.at[parity, ch], 4 + 4 * parity + ch, self.far
        )

    def total(self, ch, parity):
        self.fars.pop(ch).wait()
        return self.far_out[ch].astype(F32) + self.far_in[parity, ch].astype(F32)

    def gather(self, key, slot, ref):
        half = ref.at[self.core]
        self.gathers[key] = self.copy(half, half, 12 + slot, self.other)

    def arrived(self, key):
        self.gathers.pop(key).wait()


def attention_forward(n, win, wout, j, i, qkv, att, probs):
    q, k, v = (dot(n, win[3 * j + c]).astype(BF16) for c in range(3))
    for c, part in enumerate((q, k, v)):
        qkv[j, c, i] = part
    key = lax.broadcasted_iota(jnp.int32, (1, PAD), 1)
    mixed = None
    for h in range(3):
        s = dot_nt(only(h, q), k) * 0.125
        s = jnp.where(key < SEQ, s, -1e30)
        e = jnp.exp(s - jnp.max(s, axis=-1, keepdims=True))
        p = e * (1.0 / jnp.sum(e, axis=-1, keepdims=True))
        probs[j, i, h] = p
        term = dot(p.astype(BF16), only(h, v))
        mixed = term if mixed is None else mixed + term
    mixed = mixed.astype(BF16)
    att[j, i] = mixed
    return dot(mixed, wout[j])


def attention_backward(du, win, wout, j, i, qkv, att, probs, stack):
    q, k, v = (qkv[j, c, i] for c in range(3))
    d_att = dot_nt(du, wout[j]).astype(BF16)
    dq = dk = dv = None
    for h in range(3):
        p = probs[j, i, h]
        dp = dot_nt(only(h, d_att), v)
        ds = (p * (dp - jnp.sum(p * dp, axis=-1, keepdims=True))).astype(BF16)
        terms = (dot(ds, only(h, k)), dot_tn(ds, only(h, q)), dot_tn(p.astype(BF16), only(h, d_att)))
        dq, dk, dv = terms if dq is None else (a + b for a, b in zip((dq, dk, dv), terms))
    parts = [(dq * 0.125).astype(BF16), (dk * 0.125).astype(BF16), dv.astype(BF16)]
    stack[i * PAD : (i + 1) * PAD] = jnp.concatenate(parts + [att[j, i]], axis=1)
    return sum(dot_nt(part, win[3 * j + c]) for c, part in enumerate(parts))


def weight_grad(g, m, left, right):
    for s in range(2):
        out = dot_tn(left[:, s * 384 : (s + 1) * 384], right).astype(BF16)
        g[m, 2 * s : 2 * s + 2] = out.reshape(2, 4, 48, D)


def head_grad(g, m, n, du, stack):
    lane = lax.broadcasted_iota(jnp.int32, (1, 256), 1)
    last = stack[:, 512:]
    zero = jnp.zeros((), BF16)
    for s in range(2):
        cut = slice(s * 384, (s + 1) * 384)
        a = dot_tn(n[:, cut], stack[:, :512]).astype(BF16)
        b = dot_tn(n[:, cut], jnp.where(lane < 64, last, zero))
        b = (b + dot_tn(du[:, cut], jnp.where(lane < 64, zero, last))).astype(BF16)
        g[m, 2 * s : 2 * s + 2, :, :, 0:512] = a.reshape(2, 4, 48, 512)
        g[m, 2 * s : 2 * s + 2, :, :, 512:] = b.reshape(2, 4, 48, 256)


def forward_kernel(
    tokens, cot, gain, bias, win, wout, m1, m2, pick, spread, gate, ein, eout,
    out_o, n0, n1, n2, du2, qkv, att, probs, act, dgelu, streams, g2, terms, ge_o,
    n3, last, buf, drow, weighted, dbuf, eact, dhid, w_in, w_out, ge,
    full, pair_out, pair_in, far_out, far_in, send, recv, local_sem, grad_sem,
):
    links = TensorLinks((full, pair_out, pair_in, far_out, far_in), (send, recv))
    core = links.core
    barrier = pltpu.get_barrier_semaphore()
    for device in (links.other, links.far):
        pl.semaphore_signal(barrier, inc=1, device_id=(links.dp, device), device_id_type=MESH)
    loads = []
    for e in range(EXPERTS):
        for c, (source, target) in enumerate(((ein, w_in), (eout, w_out))):
            load = pltpu.make_async_copy(source.at[e], target.at[e], local_sem.at[2 * e + c])
            load.start()
            loads.append(load)

    def norm_rows(s, v):
        return (normalize(v)[0] * gain[s : s + 1] + bias[s : s + 1]).astype(BF16)

    for i in range(2):
        for half in range(2):
            n0[i, half] = norm_rows(0, tokens[i, half].astype(F32))
        streams[0, i] = tokens[i, core].astype(F32)

    def rows(ref, i):
        return ref[i].reshape(PAD, D)

    def block(s, i):
        if s != 1:
            return attention_forward(rows((n0, None, n2)[s], i), win, wout, s // 2, i, qkv, att, probs)
        hidden = dot(rows(n1, i), m1[...])
        act[i], dgelu[i] = gelu_pair(hidden)
        return dot(act[i], m2[...])

    normed = (n0, n1, n2, n3)

    def finish(s, i):
        v = streams[s, i] + links.total(i, s % 2)
        if s < 2:
            streams[s + 1, i] = v
        else:
            last[i] = v
        normed[s + 1][i, core] = norm_rows(s + 1, v)
        links.gather((s, i), 2 * s + i, normed[s + 1].at[i])

    steps = [(s, i) for s in range(3) for i in range(2)]
    for at, (s, i) in enumerate(steps):
        if s > 0:
            links.arrived((s - 1, i))
        term = block(s, i)
        if at == 0:
            pl.semaphore_wait(barrier, 2)
        links.share(i, term)
        links.swap(i, s % 2)
        if at > 0:
            finish(*steps[at - 1])
    finish(*steps[-1])

    drow[...] = (dot(pick[...], cot[...].reshape(2 * PAD, D)) * gate[...]).astype(BF16)
    for load in loads:
        load.wait()
    for i in range(2):
        links.arrived((2, i))
    buf[...] = dot(pick[...], n3[...].reshape(2 * PAD, D)).astype(BF16)
    for e in range(EXPERTS):
        cut = pl.ds(e * SLOTS, SLOTS)
        a, slope = gelu_pair(dot(buf[cut], w_in[e]))
        eact[cut] = a
        weighted[cut] = (dot(a, w_out[e]) * gate[cut]).astype(BF16)
        d = (slope * dot_nt(drow[cut], w_out[e])).astype(BF16)
        dhid[cut] = d
        dbuf[cut] = dot_nt(d, w_in[e]).astype(BF16)
    for i in range(2):
        links.share(i, dot(spread[i], dbuf[...]))
    for i in range(2):
        links.swap(i, 1)
    for i in range(2):
        links.share(2 + i, dot(spread[i], weighted[...]))
    for i in range(2):
        links.swap(2 + i, 1)
    copies = []

    def expert_grads(e):
        cut = pl.ds(e * SLOTS, SLOTS)
        for m, left, right in ((e, buf, dhid), (EXPERTS + e, drow, eact)):
            weight_grad(ge, m, left[cut], right[cut])
            copy = pltpu.make_async_copy(ge.at[m], ge_o.at[m], grad_sem.at[m])
            copy.start()
            copies.append(copy)

    expert_grads(0)
    expert_grads(1)
    gains = biases = 0.0
    for i in range(2):
        dv, gain_term, bias_term = norm_back(last[i], gain[3:4], links.total(i, 1))
        gains, biases = gains + gain_term, biases + bias_term
        g = cot[i, core].astype(F32) + dv
        g2[i] = g
        du2[i, core] = g.astype(BF16)
        links.gather((3, i), 6 + i, du2.at[i])
    terms[...] = jnp.zeros_like(terms)
    terms[3:4] = gains
    terms[7:8] = biases
    for i in range(2):
        out_o[i, core] = last[i] + links.total(2 + i, 1)
        links.gather((4, i), 8 + i, out_o.at[i])
    expert_grads(2)
    expert_grads(3)
    for i in range(2):
        links.arrived((3, i))
        links.arrived((4, i))
    for copy in copies:
        copy.wait()


class ImageSum:
    def __init__(self, spec, refs, sems, base, place, out):
        self.mats, self.width, self.order, self.ring, self.held = spec
        self.refs, self.sems, self.base, self.place, self.out = refs, sems, base, place, out
        self.copies = {}

    def send(self, name, slot, source, target, axis, k):
        y, z, x, t = self.place
        if axis == "x":
            device = grid_device(y, z, 1 - x)
        else:
            device = grid_device(y + k, z, x) if axis == "y" else grid_device(y, z + k, x)
        send, recv = self.sems
        c = pltpu.make_async_remote_copy(
            src_ref=source,
            dst_ref=target,
            send_sem=send.at[self.base + slot],
            recv_sem=recv.at[self.base + slot],
            device_id=(device, t),
            device_id_type=MESH,
        )
        c.start()
        self.copies.setdefault(name, []).append(c)

    def wait(self, name):
        for c in self.copies.pop(name, []):
            c.wait()

    def block(self, k):
        source, y, z = self.source, self.place[0], self.place[1]
        if self.order == "y":
            return source.at[:, lax.rem(y + k, 4)]
        return source.at[:, :, lax.rem(z + k, 4)]

    def start(self, source):
        self.source = source
        axis, h = self.order, self.width // 2
        r = self.refs
        low, high = pl.ds(0, h), pl.ds(h, h)
        if self.ring:
            far = self.block(2)
            self.send("a", 0, far.at[:, :, :, low], r["ra"].at[0], axis, 1)
            self.send("a", 1, far.at[:, :, :, high], r["ra"].at[1], axis, 3)
            self.send("b", 2, self.block(1).at[:, :, :, high], r["rb"].at[0, :, :, :, high], axis, 1)
            self.send("b", 3, self.block(3).at[:, :, :, low], r["rb"].at[1, :, :, :, low], axis, 3)
        else:
            for k in (2, 1, 3):
                self.send("b", k, self.block(k), r["rb"].at[k - 1], axis, k)
        if not self.held:
            y, z, x, t = self.place
            pieces = [
                (self.block(0), r["own"]),
                (self.block(1).at[:, :, :, low], r["near"].at[0]),
                (self.block(3).at[:, :, :, high], r["near"].at[1]),
            ]
            for i, (a, b) in enumerate(pieces):
                c = pltpu.make_async_copy(a, b, r["local"].at[i])
                c.start()
                self.copies.setdefault("own", []).append(c)

    def middle(self):
        r, h = self.refs, self.width // 2
        low, high = pl.ds(0, h), pl.ds(h, h)
        self.wait("a")
        self.wait("own")
        for side, k, cut in ((0, 1, low), (1, 3, high)):
            near = r["near"].at[side] if not self.held else self.block(k).at[:, :, :, cut]

            def add(m, carry, near=near, side=side):
                for b in range(4):
                    r["ra"][side, m, b] = (r["ra"][side, m, b].astype(F32) + near[m, b].astype(F32)).astype(BF16)
                return carry

            lax.fori_loop(0, self.mats, add, 0)
        self.send("b", 4, r["ra"].at[0], r["rb"].at[0, :, :, :, low], self.order, 1)
        self.send("b", 5, r["ra"].at[1], r["rb"].at[1, :, :, :, high], self.order, 3)

    def second(self):
        r = self.refs
        self.wait("b")
        own = self.block(0) if self.held else r["own"]

        def add(m, carry):
            for b in range(4):
                acc = own[m, b].astype(F32)
                for k in range(2 if self.ring else 3):
                    acc = acc + r["rb"][k, m, b].astype(F32)
                r["s1"][m, b] = acc.astype(BF16)
            return carry

        lax.fori_loop(0, self.mats, add, 0)
        axis = "z" if self.order == "y" else "y"
        mine = self.place[1] if axis == "z" else self.place[0]
        for k in (2, 1, 3):
            self.send("c", 5 + k, r["s1"].at[:, lax.rem(mine + k, 4)], r["rc"].at[k - 1], axis, k)

    def third(self):
        r = self.refs
        y, z, x, t = self.place
        mine = z if self.order == "y" else y
        self.wait("c")
        other = pl.ds(pl.multiple_of((1 - x) * 24, 8), 24)
        for m in range(self.mats):
            acc = r["s1"][m, mine].astype(F32)
            for k in range(3):
                acc = acc + r["rc"][k, m].astype(F32)
            r["tot"][m] = acc
        for m in range(0, self.mats, 2):
            pieces = [r["tot"][n, other] for n in (m, min(m + 1, self.mats - 1))]
            r["xs"][m // 2] = jnp.concatenate(pieces, axis=0).astype(BF16)
        self.send("d", 9, r["xs"], r["xr"], "x", 0)

    def finish(self):
        r = self.refs
        x = self.place[2]
        self.wait("d")
        mine = pl.ds(pl.multiple_of(x * 24, 8), 24)
        for m in range(self.mats):
            theirs = r["xr"][m // 2].astype(F32)
            self.out(m, r["tot"][m, mine] + theirs[24 * (m % 2) : 24 * (m % 2) + 24])


GROUPS = {
    "e0": (4, 768, "y", True, False),
    "e1": (4, 768, "z", True, False),
    "m0": (1, 768, "y", True, True),
    "m1": (1, 768, "z", True, True),
    "a1y": (1, 384, "y", False, True),
    "a1z": (1, 384, "z", False, True),
    "a0y": (1, 384, "y", False, True),
    "a0z": (1, 384, "z", False, True),
    "n": (1, 128, "y", False, True),
}


def group_scratch(spec):
    mats, width, order, ring, held = spec
    pairs = (mats + 1) // 2
    shapes = {
        "rb": pltpu.VMEM((2 if ring else 3, mats, 4, 48, width), BF16),
        "s1": pltpu.VMEM((mats, 4, 48, width), BF16),
        "rc": pltpu.VMEM((3, mats, 48, width), BF16),
        "tot": pltpu.VMEM((mats, 48, width), F32),
        "xs": pltpu.VMEM((pairs, 48, width), BF16),
        "xr": pltpu.VMEM((pairs, 48, width), BF16),
    }
    if ring:
        shapes["ra"] = pltpu.VMEM((2, mats, 4, 48, width // 2), BF16)
    if not held:
        shapes["own"] = pltpu.VMEM((mats, 4, 48, width), BF16)
        shapes["near"] = pltpu.VMEM((2, mats, 4, 48, width // 2), BF16)
        shapes["local"] = pltpu.SemaphoreType.DMA((3,))
    return shapes


BACK_IN = 18


def backward_kernel(*refs):
    (
        n0, n1, n2, du2, qkv, att, probs, act, dgelu, streams, g2, terms,
        gain, win, wout, m1, m2, ge,
    ) = refs[:BACK_IN]
    token_o, e_o, d_o, norm_o = refs[BACK_IN : BACK_IN + 4]
    rest = list(refs[BACK_IN + 4 :])
    (
        du1, du0, stack, dhid, g, gn, sums, sums_in, full, pair_out, pair_in, far_out, far_in,
        send, recv, group_send, group_recv,
    ) = rest[:17]
    rest = rest[17:]
    links = TensorLinks((full, pair_out, pair_in, far_out, far_in), (send, recv))
    core = links.core
    dp = links.dp
    t = lax.axis_index("tensor")
    y, z, x = dp // 8, lax.rem(dp // 2, 4), lax.rem(dp, 2)
    place = (y, z, x, t)

    def out_at(ref, base, cut):
        def store(m, value):
            ref[base + m, :, cut] = value

        return store

    everything = slice(None)
    outs = {
        "e0": out_at(e_o, 0, everything),
        "e1": out_at(e_o, 4, everything),
        "m0": out_at(d_o, 0, everything),
        "m1": out_at(d_o, 1, everything),
        "a1y": out_at(d_o, 3, slice(0, 384)),
        "a1z": out_at(d_o, 3, slice(384, 768)),
        "a0y": out_at(d_o, 2, slice(0, 384)),
        "a0z": out_at(d_o, 2, slice(384, 768)),
        "n": out_at(norm_o, 0, everything),
    }
    groups = {}
    for at, (name, spec) in enumerate(GROUPS.items()):
        keys = list(group_scratch(spec))
        held = dict(zip(keys, rest[: len(keys)]))
        rest = rest[len(keys) :]
        groups[name] = ImageSum(spec, held, (group_send, group_recv), 10 * at, place, outs[name])

    barrier = pltpu.get_barrier_semaphore()
    for device in ((dp, links.other), (dp, links.far), (grid_device(y, z, 1 - x), t)):
        pl.semaphore_signal(barrier, inc=1, device_id=device, device_id_type=MESH)
    for k in (1, 2, 3):
        for device in (grid_device(y + k, z, x), grid_device(y, z + k, x)):
            pl.semaphore_signal(barrier, inc=1, device_id=(device, t), device_id_type=MESH)
    pl.semaphore_wait(barrier, 9)

    groups["e0"].start(ge.at[0:4])
    groups["e1"].start(ge.at[4:8])
    sums[...] = terms[...]

    def rows(ref, i):
        return ref[i].reshape(PAD, D)

    def flat(ref):
        return ref[...].reshape(2 * PAD, D)

    def share(parity, i, value):
        links.share(i, value)
        links.swap(i, parity)

    def finish(s, parity, i, target, slot):
        dv, gain_term, bias_term = norm_back(streams[s, i], gain[s : s + 1], links.total(i, parity))
        sums[s : s + 1] = sums[s : s + 1] + gain_term
        sums[4 + s : 5 + s] = sums[4 + s : 5 + s] + bias_term
        v = g2[i] + dv
        if s > 0:
            g2[i] = v
            target[i, core] = v.astype(BF16)
        else:
            target[i, core] = v
        links.gather((s, i), 2 * s + slot, target.at[i])

    for i in range(2):
        share(0, i, attention_backward(rows(du2, i), win, wout, 1, i, qkv, att, probs, stack))
    head_grad(g, 3, flat(n2), flat(du2), stack)
    groups["a1y"].start(g.at[3:4, :, :, :, 0:384])
    groups["a1z"].start(g.at[3:4, :, :, :, 384:768])
    for i in range(2):
        finish(2, 0, i, du1, i)

    for i in range(2):
        links.arrived((2, i))
        d = (dgelu[i] * dot_nt(rows(du1, i), m2[...])).astype(BF16)
        dhid[i] = d
        share(1, i, dot_nt(d, m1[...]))
    weight_grad(g, 0, flat(n1), dhid[...].reshape(2 * PAD, D))
    groups["m0"].start(g.at[0:1])
    weight_grad(g, 1, flat(du1), act[...].reshape(2 * PAD, D))
    groups["m1"].start(g.at[1:2])
    for i in range(2):
        finish(1, 1, i, du0, i)

    for i in range(2):
        links.arrived((1, i))
        share(0, i, attention_backward(rows(du0, i), win, wout, 0, i, qkv, att, probs, stack))
    groups["e0"].middle()
    groups["e1"].middle()
    head_grad(g, 2, flat(n0), flat(du0), stack)
    groups["a0y"].start(g.at[2:3, :, :, :, 0:384])
    groups["a0z"].start(g.at[2:3, :, :, :, 384:768])
    for i in range(2):
        finish(0, 0, i, token_o, i)
    both = links.copy(sums, sums_in, 18, links.other)
    groups["a1y"].second()
    groups["a1z"].second()
    groups["m0"].middle()
    groups["m1"].middle()
    both.wait()
    wide = jnp.concatenate([sums[...] + sums_in[...], jnp.zeros((120, D), F32)], axis=0)
    gn[0] = wide.T.astype(BF16).reshape(4, 4, 48, 128)
    groups["n"].start(gn)
    for name in ("e0", "e1", "a0y", "a0z", "m0", "m1", "n"):
        groups[name].second()
    for name in ("a1y", "a1z", "e0", "e1", "a0y", "a0z", "m0", "m1", "n"):
        groups[name].third()
    for name in ("a1y", "a1z", "e0", "e1", "a0y", "a0z", "m0", "m1", "n"):
        groups[name].finish()
    for i in range(2):
        links.arrived((0, i))


def link_scratch(channels, sems):
    return [
        pltpu.VMEM((channels, 2, HALF, D), F32),
        pltpu.VMEM((channels, HALF, D), BF16),
        pltpu.VMEM((channels, HALF, D), BF16),
        pltpu.VMEM((channels, HALF, D), BF16),
        pltpu.VMEM((2, channels, HALF, D), BF16),
        pltpu.SemaphoreType.DMA((sems,)),
        pltpu.SemaphoreType.DMA((sems,)),
    ]


def padded(v):
    v = v.reshape(2, SEQ, -1)
    v = jnp.pad(v, ((0, 0), (0, PAD - SEQ), (0, 0)))
    return v.reshape(2, 2, HALF, v.shape[-1])


def unpadded(v):
    return v.reshape(2, PAD, D)[:, :SEQ].reshape(2 * SEQ, D)


def local(
    tokens,
    norm_gain,
    norm_bias,
    attn_in,
    attn_out,
    mlp_in,
    mlp_out,
    expert_in,
    expert_out,
    routes,
    slot_index,
    gate_weights,
    cotangent,
):
    head_width = attn_out.shape[1]
    kept = slot_index < CAPACITY
    index = jnp.where(kept, routes * SLOTS + slot_index, -1)
    index = jnp.pad(index.reshape(2, SEQ, 2), ((0, 0), (0, PAD - SEQ), (0, 0)), constant_values=-1)
    gates = jnp.pad(gate_weights.reshape(2, SEQ, 2), ((0, 0), (0, PAD - SEQ), (0, 0)))
    slots = EXPERTS * SLOTS
    flat = index.reshape(2 * PAD, 2)
    number = lax.broadcasted_iota(jnp.int32, (slots, 2 * PAD), 0)
    hits = [number == flat[:, k][None, :] for k in range(2)]
    pick = jnp.logical_or(*hits).astype(BF16)
    gate = sum(
        jnp.sum(jnp.where(hits[k], gates.reshape(2 * PAD, 2)[:, k][None, :], 0.0), axis=1, keepdims=True)
        for k in range(2)
    )
    number = lax.broadcasted_iota(jnp.int32, (2, PAD, slots), 2)
    spread = jnp.logical_or(number == index[:, :, :1], number == index[:, :, 1:]).astype(BF16)

    whole = pl.BlockSpec(memory_space=pltpu.VMEM)
    hbm = pl.BlockSpec(memory_space=pl.ANY)
    shape = jax.ShapeDtypeStruct
    half_rows = (2, 2, HALF, D)
    win = attn_in.reshape(6, D, head_width)
    (out, n0, n1, n2, du2, qkv, att, probs, act, dgelu, streams, g2, terms, ge) = pl.pallas_call(
        forward_kernel,
        out_shape=[
            shape(half_rows, F32),
            shape(half_rows, BF16),
            shape(half_rows, BF16),
            shape(half_rows, BF16),
            shape(half_rows, BF16),
            shape((2, 3, 2, PAD, head_width), BF16),
            shape((2, 2, PAD, head_width), BF16),
            shape((2, 2, 3, PAD, PAD), F32),
            shape((2, PAD, D), BF16),
            shape((2, PAD, D), F32),
            shape((3, 2, HALF, D), F32),
            shape((2, HALF, D), F32),
            shape((8, D), F32),
            shape((2 * EXPERTS, 4, 4, 48, D), BF16),
        ],
        in_specs=[whole] * 11 + [hbm] * 2,
        out_specs=[whole] * 13 + [hbm],
        scratch_shapes=[
            pltpu.VMEM(half_rows, BF16),
            pltpu.VMEM((2, HALF, D), F32),
        ]
        + [pltpu.VMEM((slots, D), BF16)] * 6
        + [
            pltpu.VMEM((EXPERTS, D, D), BF16),
            pltpu.VMEM((EXPERTS, D, D), BF16),
            pltpu.VMEM((2 * EXPERTS, 4, 4, 48, D), BF16),
        ]
        + link_scratch(4, 22)
        + [pltpu.SemaphoreType.DMA((8,)), pltpu.SemaphoreType.DMA((8,))],
        compiler_params=pltpu.CompilerParams(
            collective_id=1, has_side_effects=True, vmem_limit_bytes=60 << 20
        ),
        name="forward",
    )(
        padded(tokens), padded(cotangent), norm_gain, norm_bias, win, attn_out, mlp_in, mlp_out,
        pick, spread, gate, expert_in, expert_out,
    )

    scratch = (
        [
            pltpu.VMEM(half_rows, BF16),
            pltpu.VMEM(half_rows, BF16),
            pltpu.VMEM((2 * PAD, D), BF16),
            pltpu.VMEM((2, PAD, D), BF16),
            pltpu.VMEM((4, 4, 4, 48, D), BF16),
            pltpu.VMEM((1, 4, 4, 48, 128), BF16),
            pltpu.VMEM((8, D), F32),
            pltpu.VMEM((8, D), F32),
        ]
        + link_scratch(2, 20)
        + [
            pltpu.SemaphoreType.DMA((10 * len(GROUPS),)),
            pltpu.SemaphoreType.DMA((10 * len(GROUPS),)),
        ]
    )
    for spec in GROUPS.values():
        scratch += list(group_scratch(spec).values())
    token_grad, experts, dense, norms = pl.pallas_call(
        backward_kernel,
        out_shape=[
            shape(half_rows, F32),
            shape((2 * EXPERTS, 24, D), F32),
            shape((4, 24, D), F32),
            shape((1, 24, 128), F32),
        ],
        in_specs=[whole] * (BACK_IN - 1) + [hbm],
        out_specs=[whole] * 4,
        scratch_shapes=scratch,
        compiler_params=pltpu.CompilerParams(
            collective_id=2, has_side_effects=True, vmem_limit_bytes=60 << 20
        ),
        name="backward",
    )(
        n0, n1, n2, du2, qkv, att, probs, act, dgelu, streams, g2, terms,
        norm_gain, win, attn_out, mlp_in, mlp_out, ge,
    )
    heads = dense[2:]
    attn_in_sum = jnp.stack(
        [heads[:, :, c * head_width : (c + 1) * head_width] for c in range(3)], axis=1
    )
    return (
        unpadded(out),
        unpadded(token_grad),
        norms[0, :, :4].T,
        norms[0, :, 4:8].T,
        attn_in_sum,
        jnp.swapaxes(heads[:, :, 3 * head_width :], 1, 2),
        dense[0],
        dense[1].T,
        experts[:EXPERTS],
        jnp.swapaxes(experts[EXPERTS:], 1, 2),
    )


def solution(mesh):
    placed = (
        P("dp", None),
        P(),
        P(),
        P(None, None, None, "tensor"),
        P(None, "tensor", None),
        P(None, "tensor"),
        P("tensor", None),
        P(None, None, "tensor"),
        P(None, "tensor", None),
        P("dp", None),
        P("dp", None),
        P("dp", None),
        P("dp", None),
    )
    return jax.shard_map(
        local,
        mesh=mesh,
        in_specs=placed,
        out_specs=(
            P("dp", None),
            P("dp", None),
            P(None, "dp"),
            P(None, "dp"),
            P(None, None, "dp", "tensor"),
            P(None, "tensor", "dp"),
            P("dp", "tensor"),
            P("tensor", "dp"),
            P(None, "dp", "tensor"),
            P(None, "tensor", "dp"),
        ),
        check_vma=False,
    )
```

```python
import functools

import jax
import jax.numpy as jnp
from jax import lax
from jax.experimental import pallas as pl
from jax.experimental.pallas import tpu as pltpu
from jax.sharding import PartitionSpec as P

D = 768
HEAD_DIM = 64
SEQ = 197
HALF = 112
PAD = 2 * HALF
CAPACITY = 168
SLOTS = 176
EXPERTS = 4
NORM_EPSILON = 1e-06
MESH = pl.DeviceIdType.MESH
F32 = jnp.float32
BF16 = jnp.bfloat16


def dot(a, b):
    return lax.dot_general(a, b, (((1,), (0,)), ((), ())), preferred_element_type=F32)


def dot_nt(a, b):
    return lax.dot_general(a, b, (((1,), (1,)), ((), ())), preferred_element_type=F32)


def dot_tn(a, b):
    return lax.dot_general(a, b, (((0,), (0,)), ((), ())), preferred_element_type=F32)


def grid_device(y, z, x):
    return (lax.rem(y + 8, 4) * 4 + lax.rem(z + 8, 4)) * 2 + x


def normalize(v):
    center = v - jnp.mean(v, axis=-1, keepdims=True)
    spread = jnp.mean(center * center, axis=-1, keepdims=True)
    scale = lax.rsqrt(spread + NORM_EPSILON)
    return center * scale, scale


def norm_back(v, gain_row, upstream):
    nhat, scale = normalize(v)
    scaled = upstream * gain_row
    mean = jnp.mean(scaled, axis=-1, keepdims=True)
    along = jnp.mean(scaled * nhat, axis=-1, keepdims=True)
    dv = (scaled - mean - nhat * along) * scale
    gain_term = jnp.sum(upstream * nhat, axis=0, keepdims=True)
    bias_term = jnp.sum(upstream, axis=0, keepdims=True)
    return dv, gain_term, bias_term


def gelu_pair(h):
    phi = 0.5 * (1.0 + lax.erf(h * 0.7071067811865476))
    density = jnp.exp(-0.5 * h * h) * 0.3989422804014327
    return (h * phi).astype(BF16), phi + h * density


def head_mask(h, width):
    lane = lax.broadcasted_iota(jnp.int32, (1, width), 1)
    return jnp.logical_and(lane >= h * HEAD_DIM, lane < (h + 1) * HEAD_DIM)


def only(h, v):
    return jnp.where(head_mask(h, v.shape[1]), v, jnp.zeros((), v.dtype))


class TensorLinks:
    def __init__(self, refs, sems):
        self.full, self.pair_out, self.pair_in, self.far_out, self.far_in = refs
        self.sems = sems
        self.dp = lax.axis_index("dp")
        t = lax.axis_index("tensor")
        self.core = lax.rem(t, 2)
        self.other = t + 1 - 2 * self.core
        self.far = lax.rem(t + 2, 4)
        self.pairs, self.fars, self.gathers, self.mine = {}, {}, {}, {}

    def copy(self, source, target, slot, device):
        send, recv = self.sems
        c = pltpu.make_async_remote_copy(
            src_ref=source,
            dst_ref=target,
            send_sem=send.at[slot],
            recv_sem=recv.at[slot],
            device_id=(self.dp, device),
            device_id_type=MESH,
        )
        c.start()
        return c

    def share(self, ch, value):
        self.full[ch, 0] = value[:HALF]
        self.full[ch, 1] = value[HALF:]
        self.pair_out[ch] = self.full[ch, 1 - self.core].astype(BF16)
        self.pairs[ch] = self.copy(self.pair_out.at[ch], self.pair_in.at[ch], ch, self.other)
        self.mine[ch] = lambda: self.full[ch, self.core]

    def share_held(self, ch, ref):
        self.pairs[ch] = self.copy(ref.at[1 - self.core], self.pair_in.at[ch], ch, self.other)
        self.mine[ch] = lambda: ref[self.core].astype(F32)

    def place(self, ch, parity):
        return 2 * parity + ch if ch < 2 else 2 + ch

    def swap(self, ch, parity):
        self.pairs.pop(ch).wait()
        mine = self.mine.pop(ch)() + self.pair_in[ch].astype(F32)
        self.far_out[ch] = mine.astype(BF16)
        at = self.place(ch, parity)
        self.fars[ch] = self.copy(self.far_out.at[ch], self.far_in.at[at], 4 + at, self.far)

    def total(self, ch, parity):
        self.fars.pop(ch).wait()
        return self.far_out[ch].astype(F32) + self.far_in[self.place(ch, parity)].astype(F32)

    def gather(self, key, slot, ref):
        half = ref.at[self.core]
        self.gathers[key] = self.copy(half, half, 10 + slot, self.other)

    def arrived(self, key):
        self.gathers.pop(key).wait()


class Loads:
    def __init__(self, sems):
        self.sems, self.pending, self.count = sems, {}, 0

    def start(self, key, source, target):
        c = pltpu.make_async_copy(source, target, self.sems.at[self.count])
        c.start()
        self.count += 1
        self.pending[key] = c

    def need(self, *keys):
        for key in keys:
            if key in self.pending:
                self.pending.pop(key).wait()

    def drain(self):
        self.need(*list(self.pending))


def attention_forward(n, win, wout, j, i, qkv, att, probs):
    q, k, v = (dot_nt(n, win[3 * j + c]).astype(BF16) for c in range(3))
    for c, part in enumerate((q, k, v)):
        qkv[j, c, i] = part
    key = lax.broadcasted_iota(jnp.int32, (1, PAD), 1)
    mixed = None
    for h in range(3):
        s = dot_nt(only(h, q), k) * 0.125
        s = jnp.where(key < SEQ, s, -1e30)
        e = jnp.exp(s - jnp.max(s, axis=-1, keepdims=True))
        p = e * (1.0 / jnp.sum(e, axis=-1, keepdims=True))
        probs[j, i, h] = p
        term = dot(p.astype(BF16), only(h, v))
        mixed = term if mixed is None else mixed + term
    mixed = mixed.astype(BF16)
    att[j, i] = mixed
    return dot(mixed, wout[j])


def attention_backward(du, win, wout, j, i, qkv, att, probs, stack):
    q, k, v = (qkv[j, c, i] for c in range(3))
    d_att = dot_nt(du, wout[j]).astype(BF16)
    dq = dk = dv = None
    for h in range(3):
        p = probs[j, i, h]
        dp = dot_nt(only(h, d_att), v)
        ds = (p * (dp - jnp.sum(p * dp, axis=-1, keepdims=True))).astype(BF16)
        terms = (dot(ds, only(h, k)), dot_tn(ds, only(h, q)), dot_tn(p.astype(BF16), only(h, d_att)))
        dq, dk, dv = terms if dq is None else (a + b for a, b in zip((dq, dk, dv), terms))
    parts = [(dq * 0.125).astype(BF16), (dk * 0.125).astype(BF16), dv.astype(BF16)]
    stack[i * PAD : (i + 1) * PAD] = jnp.concatenate(parts + [att[j, i]], axis=1)
    return sum(dot(part, win[3 * j + c]) for c, part in enumerate(parts))


def weight_grad(g, m, left, right):
    for s in range(2):
        out = dot_tn(left[:, s * 384 : (s + 1) * 384], right).astype(BF16)
        g[m, 2 * s : 2 * s + 2] = out.reshape(2, 4, 48, D)


def head_grad(g, m, n, du, stack):
    lane = lax.broadcasted_iota(jnp.int32, (1, 256), 1)
    last = stack[:, 512:]
    zero = jnp.zeros((), BF16)
    for s in range(2):
        cut = slice(s * 384, (s + 1) * 384)
        a = dot_tn(n[:, cut], stack[:, :512]).astype(BF16)
        b = dot_tn(n[:, cut], jnp.where(lane < 64, last, zero))
        b = (b + dot_tn(du[:, cut], jnp.where(lane < 64, zero, last))).astype(BF16)
        g[m, 2 * s : 2 * s + 2, :, :, 0:512] = a.reshape(2, 4, 48, 512)
        g[m, 2 * s : 2 * s + 2, :, :, 512:] = b.reshape(2, 4, 48, 256)


KEPT = ("n0", "n1", "n2", "cotp", "qkv", "att", "probs", "act", "dgelu", "streams", "dn", "mo")


def kept_shapes(head_width):
    half_rows = (2, 2, HALF, D)
    return {
        "n0": (half_rows, BF16),
        "n1": (half_rows, BF16),
        "n2": (half_rows, BF16),
        "cotp": (half_rows, BF16),
        "qkv": ((2, 3, 2, PAD, head_width), BF16),
        "att": ((2, 2, PAD, head_width), BF16),
        "probs": ((2, 2, 3, PAD, PAD), F32),
        "act": ((2, PAD, D), BF16),
        "dgelu": ((2, PAD, D), F32),
        "streams": ((4, 2, HALF, D), F32),
        "dn": (half_rows, BF16),
        "mo": (half_rows, BF16),
    }


def forward_kernel(
    tokens, cot, routes, slots, gates, gain, bias, win, wout, m1_h, m2_h, ein, eout, *refs
):
    outs = dict(zip(KEPT, refs))
    ge_o = refs[len(KEPT)]
    refs = refs[len(KEPT) + 1 :]
    kept = dict(zip(KEPT, refs))
    (
        n3, pick, spread, gate, buf, drow, weighted, dbuf, eact, dhid, m1, m2, w_in, w_out, ge,
        full, pair_out, pair_in, far_out, far_in, send, recv, load_sem, save_sem,
    ) = refs[len(KEPT) :]
    n0, n1, n2, cotp, qkv, att, probs, act, dgelu, streams, dn, mo = (kept[k] for k in KEPT)
    links = TensorLinks((full, pair_out, pair_in, far_out, far_in), (send, recv))
    core = links.core
    barrier = pltpu.get_barrier_semaphore()
    for device in (links.other, links.far):
        pl.semaphore_signal(barrier, inc=1, device_id=(links.dp, device), device_id_type=MESH)
    loads, saves = Loads(load_sem), Loads(save_sem)
    loads.start("m1", m1_h, m1)
    loads.start("m2", m2_h, m2)
    for e in range(EXPERTS):
        loads.start(("in", e), ein.at[e], w_in.at[e])
        loads.start(("out", e), eout.at[e], w_out.at[e])

    rows_of = tokens.shape[0]

    def placement():
        row = lax.broadcasted_iota(jnp.int32, (2 * PAD, rows_of), 0)
        column = lax.broadcasted_iota(jnp.int32, (2 * PAD, rows_of), 1)
        image = (row >= PAD).astype(jnp.int32)
        inside = row - image * PAD < SEQ
        hit = jnp.logical_and(inside, column == row - image * (PAD - SEQ))
        return jnp.where(hit, 1.0, 0.0).astype(BF16)

    def padded(ref):
        return dot(placement(), ref[...]).astype(BF16).reshape(2, 2, HALF, D)

    def norm_rows(s, v):
        return (normalize(v)[0] * gain[s : s + 1] + bias[s : s + 1]).astype(BF16)

    mo[...] = padded(tokens)
    for i in range(2):
        for half in range(2):
            n0[i, half] = norm_rows(0, mo[i, half].astype(F32))
        streams[0, i] = mo[i, core].astype(F32)

    def rows(ref, i):
        return ref[i].reshape(PAD, D)

    def block(s, i):
        if s != 1:
            return attention_forward(rows((n0, None, n2)[s], i), win, wout, s // 2, i, qkv, att, probs)
        loads.need("m1", "m2")
        hidden = dot(rows(n1, i), m1[...])
        act[i], dgelu[i] = gelu_pair(hidden)
        return dot(act[i], m2[...])

    normed = (n0, n1, n2, n3)

    def finish(s, i):
        v = streams[s, i] + links.total(i, s % 2)
        streams[s + 1, i] = v
        normed[s + 1][i, core] = norm_rows(s + 1, v)
        links.gather((s, i), 2 * s + i, normed[s + 1].at[i])

    def hits():
        kept_choice = slots[...] < CAPACITY
        index = jnp.where(kept_choice, routes[...] * SLOTS + slots[...], -1)
        number = lax.broadcasted_iota(jnp.int32, (EXPERTS * SLOTS, rows_of), 0)
        return [number == index[k : k + 1] for k in range(2)]

    def make_pick():
        first, second = hits()
        flat = jnp.where(jnp.logical_or(first, second), 1.0, 0.0).astype(BF16)
        pick[...] = dot_nt(flat, placement()).astype(BF16)

    def make_spread():
        first, second = hits()
        flat = jnp.where(jnp.logical_or(first, second), 1.0, 0.0).astype(BF16)
        spread[...] = dot_nt(placement(), flat).astype(BF16)

    def make_gate():
        gate[...] = sum(
            jnp.sum(jnp.where(hit, gates[k : k + 1], 0.0), axis=1, keepdims=True)
            for k, hit in enumerate(hits())
        )

    def make_cot():
        cotp[...] = padded(cot)

    def make_drow():
        drow[...] = (dot(pick[...], cotp[...].reshape(2 * PAD, D)) * gate[...]).astype(BF16)

    fill = (make_pick, make_spread, make_gate, make_cot, make_drow, None)
    steps = [(s, i) for s in range(3) for i in range(2)]
    for at, (s, i) in enumerate(steps):
        if s > 0:
            links.arrived((s - 1, i))
        term = block(s, i)
        if at == 0:
            pl.semaphore_wait(barrier, 2)
        links.share(i, term)
        if fill[at] is not None:
            fill[at]()
        links.swap(i, s % 2)
        if at > 0:
            finish(*steps[at - 1])
    for key in KEPT[:9]:
        saves.start(key, kept[key], outs[key])
    finish(*steps[-1])
    saves.start("streams", streams, outs["streams"])

    loads.drain()
    for i in range(2):
        links.arrived((2, i))
    buf[...] = dot(pick[...], n3[...].reshape(2 * PAD, D)).astype(BF16)
    for e in range(EXPERTS):
        cut = pl.ds(e * SLOTS, SLOTS)
        a, slope = gelu_pair(dot(buf[cut], w_in[e]))
        eact[cut] = a
        weighted[cut] = (dot(a, w_out[e]) * gate[cut]).astype(BF16)
        d = (slope * dot_nt(drow[cut], w_out[e])).astype(BF16)
        dhid[cut] = d
        dbuf[cut] = dot_nt(d, w_in[e]).astype(BF16)
        for m, left, right in ((e, buf, dhid), (EXPERTS + e, drow, eact)):
            weight_grad(ge, m, left[cut], right[cut])
            saves.start(("ge", m), ge.at[m], ge_o.at[m])
    dn[...] = dot(spread[...], dbuf[...]).astype(BF16).reshape(2, 2, HALF, D)
    saves.start("dn", dn, outs["dn"])
    mo[...] = dot(spread[...], weighted[...]).astype(BF16).reshape(2, 2, HALF, D)
    saves.start("mo", mo, outs["mo"])
    saves.drain()


class ImageSum:
    def __init__(self, spec, refs, sems, base, place, out):
        self.mats, self.width, self.order, self.ring, self.held = spec
        self.refs, self.sems, self.base, self.place, self.out = refs, sems, base, place, out
        self.copies = {}

    def send(self, name, slot, source, target, axis, k):
        y, z, x, t = self.place
        if axis == "x":
            device = grid_device(y, z, 1 - x)
        else:
            device = grid_device(y + k, z, x) if axis == "y" else grid_device(y, z + k, x)
        send, recv = self.sems
        c = pltpu.make_async_remote_copy(
            src_ref=source,
            dst_ref=target,
            send_sem=send.at[self.base + slot],
            recv_sem=recv.at[self.base + slot],
            device_id=(device, t),
            device_id_type=MESH,
        )
        c.start()
        self.copies.setdefault(name, []).append(c)

    def wait(self, name):
        for c in self.copies.pop(name, []):
            c.wait()

    def block(self, k):
        source, y, z = self.source, self.place[0], self.place[1]
        if self.order == "y":
            return source.at[:, lax.rem(y + k, 4)]
        return source.at[:, :, lax.rem(z + k, 4)]

    def start(self, source):
        self.source = source
        axis, h = self.order, self.width // 2
        r = self.refs
        low, high = pl.ds(0, h), pl.ds(h, h)
        if self.ring:
            far = self.block(2)
            self.send("a", 0, far.at[:, :, :, low], r["ra"].at[0], axis, 1)
            self.send("a", 1, far.at[:, :, :, high], r["ra"].at[1], axis, 3)
            self.send("b", 2, self.block(1).at[:, :, :, high], r["rb"].at[0, :, :, :, high], axis, 1)
            self.send("b", 3, self.block(3).at[:, :, :, low], r["rb"].at[1, :, :, :, low], axis, 3)
        else:
            for k in (2, 1, 3):
                self.send("b", k, self.block(k), r["rb"].at[k - 1], axis, k)
        if not self.held:
            y, z, x, t = self.place
            pieces = [
                (self.block(0), r["own"]),
                (self.block(1).at[:, :, :, low], r["near"].at[0]),
                (self.block(3).at[:, :, :, high], r["near"].at[1]),
            ]
            for i, (a, b) in enumerate(pieces):
                c = pltpu.make_async_copy(a, b, r["local"].at[i])
                c.start()
                self.copies.setdefault("own", []).append(c)

    def middle(self):
        r, h = self.refs, self.width // 2
        low, high = pl.ds(0, h), pl.ds(h, h)
        self.wait("a")
        self.wait("own")
        for side, k, cut in ((0, 1, low), (1, 3, high)):
            near = r["near"].at[side] if not self.held else self.block(k).at[:, :, :, cut]

            def add(m, carry, near=near, side=side):
                for b in range(4):
                    r["ra"][side, m, b] = (r["ra"][side, m, b].astype(F32) + near[m, b].astype(F32)).astype(BF16)
                return carry

            lax.fori_loop(0, self.mats, add, 0)
        self.send("b", 4, r["ra"].at[0], r["rb"].at[0, :, :, :, low], self.order, 1)
        self.send("b", 5, r["ra"].at[1], r["rb"].at[1, :, :, :, high], self.order, 3)

    def second(self):
        r = self.refs
        self.wait("b")
        own = self.block(0) if self.held else r["own"]
        s1 = r["s1"] if self.held else own

        def add(m, carry):
            for b in range(4):
                acc = own[m, b].astype(F32)
                for k in range(2 if self.ring else 3):
                    acc = acc + r["rb"][k, m, b].astype(F32)
                s1[m, b] = acc.astype(BF16)
            return carry

        lax.fori_loop(0, self.mats, add, 0)
        axis = "z" if self.order == "y" else "y"
        mine = self.place[1] if axis == "z" else self.place[0]
        for k in (2, 1, 3):
            self.send("c", 5 + k, s1.at[:, lax.rem(mine + k, 4)], r["rc"].at[k - 1], axis, k)

    def third(self):
        r = self.refs
        y, z, x, t = self.place
        mine = z if self.order == "y" else y
        self.wait("c")
        other = pl.ds(pl.multiple_of((1 - x) * 24, 8), 24)
        for m in range(self.mats):
            acc = r["s1" if self.held else "own"][m, mine].astype(F32)
            for k in range(3):
                acc = acc + r["rc"][k, m].astype(F32)
            r["tot"][m] = acc
        for m in range(0, self.mats, 2):
            pieces = [r["tot"][n, other] for n in (m, min(m + 1, self.mats - 1))]
            r["xs"][m // 2] = jnp.concatenate(pieces, axis=0).astype(BF16)
        self.send("d", 9, r["xs"], r["xr"], "x", 0)

    def finish(self):
        r = self.refs
        x = self.place[2]
        self.wait("d")
        mine = pl.ds(pl.multiple_of(x * 24, 8), 24)
        for m in range(self.mats):
            theirs = r["xr"][m // 2].astype(F32)
            self.out(m, r["tot"][m, mine] + theirs[24 * (m % 2) : 24 * (m % 2) + 24])


GROUPS = {
    "e0": (4, 768, "y", True, False),
    "e1": (4, 768, "z", True, False),
    "m0": (1, 768, "y", True, True),
    "m1": (1, 768, "z", True, True),
    "a1y": (1, 384, "y", False, True),
    "a1z": (1, 384, "z", False, True),
    "a0y": (1, 384, "y", False, True),
    "a0z": (1, 384, "z", False, True),
    "n": (1, 128, "y", False, True),
}


def group_scratch(spec):
    mats, width, order, ring, held = spec
    pairs = (mats + 1) // 2
    shapes = {
        "rb": pltpu.VMEM((2 if ring else 3, mats, 4, 48, width), BF16),
        "s1" if held else "own": pltpu.VMEM((mats, 4, 48, width), BF16),
        "rc": pltpu.VMEM((3, mats, 48, width), BF16),
        "tot": pltpu.VMEM((mats, 48, width), F32),
        "xs": pltpu.VMEM((pairs, 48, width), BF16),
        "xr": pltpu.VMEM((pairs, 48, width), BF16),
    }
    if ring:
        shapes["ra"] = pltpu.VMEM((2, mats, 4, 48, width // 2), BF16)
    if not held:
        shapes["near"] = pltpu.VMEM((2, mats, 4, 48, width // 2), BF16)
        shapes["local"] = pltpu.SemaphoreType.DMA((3,))
    return shapes


def backward_kernel(*refs):
    hbm = dict(zip(KEPT, refs))
    gain, ge, win_h, wout_h, m1_h, m2_h = refs[len(KEPT) : len(KEPT) + 6]
    refs = refs[len(KEPT) + 6 :]
    (
        out_o, token_o, gain_o, bias_o, heads_in_o, heads_out_o, m_in_o, m_out_o, e_in_o, e_out_o,
    ) = refs[:10]
    kept = dict(zip(KEPT, refs[10:]))
    rest = refs[10 + len(KEPT) :]
    (
        win, wout, m1, m2, outp, tokenp, g2, du2, du1, du0, stack, dhid, g, gn, sums, sums_in,
        full, pair_out, pair_in, far_out, far_in,
        send, recv, group_send, group_recv, load_sem,
    ) = rest[:26]
    rest = rest[26:]
    n0, n1, n2, cotp, qkv, att, probs, act, dgelu, streams, dn, mo = (kept[k] for k in KEPT)
    links = TensorLinks((full, pair_out, pair_in, far_out, far_in), (send, recv))
    core = links.core
    dp = links.dp
    t = lax.axis_index("tensor")
    y, z, x = dp // 8, lax.rem(dp // 2, 4), lax.rem(dp, 2)
    place = (y, z, x, t)

    barrier = pltpu.get_barrier_semaphore()
    for device in ((dp, links.other), (dp, links.far), (grid_device(y, z, 1 - x), t)):
        pl.semaphore_signal(barrier, inc=1, device_id=device, device_id_type=MESH)
    for k in (1, 2, 3):
        for device in (grid_device(y + k, z, x), grid_device(y, z + k, x)):
            pl.semaphore_signal(barrier, inc=1, device_id=(device, t), device_id_type=MESH)
    loads = Loads(load_sem)
    weights = {"win": (win_h, win), "wout": (wout_h, wout), "m1": (m1_h, m1), "m2": (m2_h, m2)}
    order = (
        "dn", "streams", "cotp", "mo", "wout", "qkv", "att", "probs", "win", "n2", "m2", "dgelu", "m1",
        "n1", "act", "n0",
    )
    for key in order:
        loads.start(key, *(weights[key] if key in weights else (hbm[key], kept[key])))

    def store(ref, *index):
        def put(m, value):
            ref[index] = value

        return put

    def store_expert(ref):
        def put(m, value):
            ref[m] = value

        return put

    def store_heads(j, first):
        def put(m, value):
            width = heads_in_o.shape[-1]
            low, high = value[:, :width], pltpu.roll(value, width, 1)[:, :width]
            if first == 0:
                heads_in_o[j, 0] = low
                heads_in_o[j, 1] = high
            else:
                heads_in_o[j, 2] = low
                heads_out_o[j] = high

        return put

    def store_norms(m, value):
        turned = jnp.concatenate([value, jnp.zeros((104, 128), F32)], axis=0).T
        gain_o[...] = turned[0:4, :24]
        bias_o[...] = turned[4:8, :24]

    outs = {
        "e0": store_expert(e_in_o),
        "e1": store_expert(e_out_o),
        "m0": store(m_in_o, Ellipsis),
        "m1": store(m_out_o, Ellipsis),
        "a1y": store_heads(1, 0),
        "a1z": store_heads(1, 384),
        "a0y": store_heads(0, 0),
        "a0z": store_heads(0, 384),
        "n": store_norms,
    }
    groups = {}
    for at, (name, spec) in enumerate(GROUPS.items()):
        keys = list(group_scratch(spec))
        held = dict(zip(keys, rest[: len(keys)]))
        rest = rest[len(keys) :]
        groups[name] = ImageSum(spec, held, (group_send, group_recv), 10 * at, place, outs[name])

    pl.semaphore_wait(barrier, 9)
    groups["e0"].start(ge.at[0:4])
    groups["e1"].start(ge.at[4:8])

    def rows(ref, i):
        return ref[i].reshape(PAD, D)

    def flat(ref):
        return ref[...].reshape(2 * PAD, D)

    def share(parity, i, value):
        links.share(i, value)
        links.swap(i, parity)

    def finish(s, parity, i, base, target, slot):
        dv, gain_term, bias_term = norm_back(streams[s, i], gain[s : s + 1], links.total(i, parity))
        sums[s : s + 1] = sums[s : s + 1] + gain_term
        sums[4 + s : 5 + s] = sums[4 + s : 5 + s] + bias_term
        v = base[i].astype(F32) + dv if s < 3 else base[i, core].astype(F32) + dv
        if s > 0:
            g2[i] = v
            target[i, core] = v.astype(BF16)
        else:
            target[i, core] = v
        links.gather((s, i), 2 * slot + i, target.at[i])

    def write_rows(ref, pad):
        for i in range(2):
            ref[i * SEQ : (i + 1) * SEQ] = pad[i].reshape(PAD, D)[:SEQ]

    sums[...] = jnp.zeros_like(sums)
    loads.need("dn")
    for i in range(2):
        links.share_held(i, dn.at[i])
    for i in range(2):
        links.swap(i, 1)
    loads.need("mo")
    for i in range(2):
        links.share_held(2 + i, mo.at[i])
    loads.need("streams", "cotp")
    for i in range(2):
        finish(3, 1, i, cotp, du2, 0)
    for i in range(2):
        links.swap(2 + i, 0)

    loads.need("wout", "qkv", "att", "probs", "win")
    for i in range(2):
        links.arrived((3, i))
        share(0, i, attention_backward(rows(du2, i), win, wout, 1, i, qkv, att, probs, stack))
    loads.need("n2")
    head_grad(g, 3, flat(n2), flat(du2), stack)
    groups["a1y"].start(g.at[3:4, :, :, :, 0:384])
    groups["a1z"].start(g.at[3:4, :, :, :, 384:768])
    for i in range(2):
        finish(2, 0, i, g2, du1, 1)
    for i in range(2):
        outp[i, core] = streams[3, i] + links.total(2 + i, 0)
        links.gather((4, i), 8 + i, outp.at[i])

    loads.need("m2", "dgelu", "m1")
    for i in range(2):
        links.arrived((2, i))
        d = (dgelu[i] * dot_nt(rows(du1, i), m2[...])).astype(BF16)
        dhid[i] = d
        share(1, i, dot_nt(d, m1[...]))
    groups["e0"].middle()
    groups["e1"].middle()
    loads.need("n1", "act")
    weight_grad(g, 0, flat(n1), dhid[...].reshape(2 * PAD, D))
    groups["m0"].start(g.at[0:1])
    weight_grad(g, 1, flat(du1), act[...].reshape(2 * PAD, D))
    groups["m1"].start(g.at[1:2])
    for i in range(2):
        finish(1, 1, i, g2, du0, 2)

    for i in range(2):
        links.arrived((1, i))
        share(0, i, attention_backward(rows(du0, i), win, wout, 0, i, qkv, att, probs, stack))
    loads.need("n0")
    head_grad(g, 2, flat(n0), flat(du0), stack)
    groups["a0y"].start(g.at[2:3, :, :, :, 0:384])
    groups["a0z"].start(g.at[2:3, :, :, :, 384:768])
    for i in range(2):
        finish(0, 0, i, g2, tokenp, 3)
    both = links.copy(sums, sums_in, 20, links.other)
    for i in range(2):
        links.arrived((4, i))
    write_rows(out_o, outp)
    both.wait()
    wide = jnp.concatenate([sums[...] + sums_in[...], jnp.zeros((120, D), F32)], axis=0)
    gn[0] = wide.T.astype(BF16).reshape(4, 4, 48, 128)
    groups["n"].start(gn)
    for name in ("m0", "m1"):
        groups[name].middle()
    for name in ("e0", "e1", "a1y", "a1z", "a0y", "a0z", "n", "m0", "m1"):
        groups[name].second()
    for i in range(2):
        links.arrived((0, i))
    write_rows(token_o, tokenp)
    for name in ("e0", "e1", "a1y", "a1z", "a0y", "a0z", "n", "m0", "m1"):
        groups[name].third()
    for name in ("e0", "e1", "a1y", "a1z", "a0y", "a0z", "n", "m0", "m1"):
        groups[name].finish()


def publish_kernel(*refs):
    count = len(refs) // 2
    sems = refs[-1]
    copies = [pltpu.make_async_copy(refs[k], refs[count + k], sems.at[k]) for k in range(count)]
    for copy in copies:
        copy.start()
    for copy in copies:
        copy.wait()


def link_scratch(channels, sems):
    return [
        pltpu.VMEM((2, 2, HALF, D), F32),
        pltpu.VMEM((2, HALF, D), BF16),
        pltpu.VMEM((channels, HALF, D), BF16),
        pltpu.VMEM((channels, HALF, D), BF16),
        pltpu.VMEM((2 + channels, HALF, D), BF16),
        pltpu.SemaphoreType.DMA((sems,)),
        pltpu.SemaphoreType.DMA((sems,)),
    ]


def local(
    tokens,
    norm_gain,
    norm_bias,
    attn_in,
    attn_out,
    mlp_in,
    mlp_out,
    expert_in,
    expert_out,
    routes,
    slot_index,
    gate_weights,
    cotangent,
):
    head_width = attn_out.shape[1]
    slots = EXPERTS * SLOTS
    rows = tokens.shape[0]
    whole = pl.BlockSpec(memory_space=pltpu.VMEM)
    hbm = pl.BlockSpec(memory_space=pl.ANY)
    shape = jax.ShapeDtypeStruct
    half_rows = (2, 2, HALF, D)
    win = jnp.swapaxes(attn_in, 2, 3).reshape(6, head_width, D)
    kept = kept_shapes(head_width)
    keeping = [pltpu.VMEM(*kept[key]) for key in KEPT]
    grads = pltpu.VMEM((2 * EXPERTS, 4, 4, 48, D), BF16)
    *stored, ge = pl.pallas_call(
        forward_kernel,
        out_shape=[shape(*kept[key]) for key in KEPT] + [shape(grads.shape, BF16)],
        in_specs=[whole] * 9 + [hbm] * 4,
        out_specs=[hbm] * (len(KEPT) + 1),
        scratch_shapes=keeping
        + [
            pltpu.VMEM(half_rows, BF16),
            pltpu.VMEM((slots, 2 * PAD), BF16),
            pltpu.VMEM((2 * PAD, slots), BF16),
            pltpu.VMEM((slots, 1), F32),
        ]
        + [pltpu.VMEM((slots, D), BF16)] * 6
        + [
            pltpu.VMEM((D, D), BF16),
            pltpu.VMEM((D, D), BF16),
            pltpu.VMEM((EXPERTS, D, D), BF16),
            pltpu.VMEM((EXPERTS, D, D), BF16),
            grads,
        ]
        + link_scratch(2, 18)
        + [pltpu.SemaphoreType.DMA((10,)), pltpu.SemaphoreType.DMA((20,))],
        compiler_params=pltpu.CompilerParams(
            collective_id=1, has_side_effects=True, vmem_limit_bytes=60 << 20
        ),
        name="forward",
    )(
        tokens, cotangent, routes.T, slot_index.T, gate_weights.T, norm_gain, norm_bias, win, attn_out,
        mlp_in, mlp_out, expert_in, expert_out,
    )

    scratch = (
        keeping
        + [
            pltpu.VMEM((6, head_width, D), BF16),
            pltpu.VMEM((2, head_width, D), BF16),
            pltpu.VMEM((D, D), BF16),
            pltpu.VMEM((D, D), BF16),
            pltpu.VMEM(half_rows, F32),
            pltpu.VMEM(half_rows, F32),
            pltpu.VMEM((2, HALF, D), F32),
            pltpu.VMEM(half_rows, BF16),
            pltpu.VMEM(half_rows, BF16),
            pltpu.VMEM(half_rows, BF16),
            pltpu.VMEM((2 * PAD, D), BF16),
            pltpu.VMEM((2, PAD, D), BF16),
            pltpu.VMEM((4, 4, 4, 48, D), BF16),
            pltpu.VMEM((1, 4, 4, 48, 128), BF16),
            pltpu.VMEM((8, D), F32),
            pltpu.VMEM((8, D), F32),
        ]
        + link_scratch(4, 22)
        + [
            pltpu.SemaphoreType.DMA((10 * len(GROUPS),)),
            pltpu.SemaphoreType.DMA((10 * len(GROUPS),)),
            pltpu.SemaphoreType.DMA((16,)),
        ]
    )
    for spec in GROUPS.values():
        scratch += list(group_scratch(spec).values())
    results = pl.pallas_call(
        backward_kernel,
        out_shape=[
            shape((rows, D), F32),
            shape((rows, D), F32),
            shape((4, 24), F32),
            shape((4, 24), F32),
            shape((2, 3, 24, head_width), F32),
            shape((2, 24, head_width), F32),
            shape((24, D), F32),
            shape((24, D), F32),
            shape((EXPERTS, 24, D), F32),
            shape((EXPERTS, 24, D), F32),
        ],
        in_specs=[hbm] * len(KEPT) + [whole] + [hbm] * 5,
        out_specs=[whole] * 10,
        scratch_shapes=scratch,
        compiler_params=pltpu.CompilerParams(
            collective_id=2, has_side_effects=True, vmem_limit_bytes=62 << 20
        ),
        name="backward",
    )(*stored, norm_gain, ge, win, attn_out, mlp_in, mlp_out)
    out, token_grad, gains, biases, heads_in, heads_out, m_in, m_out, e_in, e_out = pl.pallas_call(
        publish_kernel,
        out_shape=[shape(r.shape, r.dtype) for r in results],
        in_specs=[hbm] * len(results),
        out_specs=[whole] * len(results),
        scratch_shapes=[pltpu.SemaphoreType.DMA((len(results),))],
        name="publish",
    )(*results)
    return (
        out,
        token_grad,
        gains,
        biases,
        heads_in,
        jnp.swapaxes(heads_out, 1, 2),
        m_in,
        m_out.T,
        e_in,
        jnp.swapaxes(e_out, 1, 2),
    )


def solution(mesh):
    placed = (
        P("dp", None),
        P(),
        P(),
        P(None, None, None, "tensor"),
        P(None, "tensor", None),
        P(None, "tensor"),
        P("tensor", None),
        P(None, None, "tensor"),
        P(None, "tensor", None),
        P("dp", None),
        P("dp", None),
        P("dp", None),
        P("dp", None),
    )
    return jax.shard_map(
        local,
        mesh=mesh,
        in_specs=placed,
        out_specs=(
            P("dp", None),
            P("dp", None),
            P(None, "dp"),
            P(None, "dp"),
            P(None, None, "dp", "tensor"),
            P(None, "tensor", "dp"),
            P("dp", "tensor"),
            P("tensor", "dp"),
            P(None, "dp", "tensor"),
            P(None, "tensor", "dp"),
        ),
        check_vma=False,
    )
```

```python
import functools

import jax
import jax.numpy as jnp
from jax import lax
from jax.experimental import pallas as pl
from jax.experimental.pallas import tpu as pltpu
from jax.sharding import PartitionSpec as P

D = 768
HEAD_DIM = 64
SEQ = 197
HALF = 112
PAD = 2 * HALF
CAPACITY = 168
SLOTS = 176
EXPERTS = 4
NORM_EPSILON = 1e-06
MESH = pl.DeviceIdType.MESH
F32 = jnp.float32
BF16 = jnp.bfloat16


def dot(a, b):
    return lax.dot_general(a, b, (((1,), (0,)), ((), ())), preferred_element_type=F32)


def dot_nt(a, b):
    return lax.dot_general(a, b, (((1,), (1,)), ((), ())), preferred_element_type=F32)


def dot_tn(a, b):
    return lax.dot_general(a, b, (((0,), (0,)), ((), ())), preferred_element_type=F32)


def grid_device(y, z, x):
    return (lax.rem(y + 8, 4) * 4 + lax.rem(z + 8, 4)) * 2 + x


def normalize(v):
    center = v - jnp.mean(v, axis=-1, keepdims=True)
    spread = jnp.mean(center * center, axis=-1, keepdims=True)
    scale = lax.rsqrt(spread + NORM_EPSILON)
    return center * scale, scale


def norm_back(v, gain_row, upstream):
    nhat, scale = normalize(v)
    scaled = upstream * gain_row
    mean = jnp.mean(scaled, axis=-1, keepdims=True)
    along = jnp.mean(scaled * nhat, axis=-1, keepdims=True)
    dv = (scaled - mean - nhat * along) * scale
    gain_term = jnp.sum(upstream * nhat, axis=0, keepdims=True)
    bias_term = jnp.sum(upstream, axis=0, keepdims=True)
    return dv, gain_term, bias_term


def gelu_pair(h):
    phi = 0.5 * (1.0 + lax.erf(h * 0.7071067811865476))
    density = jnp.exp(-0.5 * h * h) * 0.3989422804014327
    return (h * phi).astype(BF16), phi + h * density


def head_mask(h, width):
    lane = lax.broadcasted_iota(jnp.int32, (1, width), 1)
    return jnp.logical_and(lane >= h * HEAD_DIM, lane < (h + 1) * HEAD_DIM)


def only(h, v):
    return jnp.where(head_mask(h, v.shape[1]), v, jnp.zeros((), v.dtype))


class TensorLinks:
    def __init__(self, refs, sems):
        self.own, self.pair_out, self.pair_in, self.far_out, self.far_in = refs
        self.sems = sems
        self.dp = lax.axis_index("dp")
        t = lax.axis_index("tensor")
        self.core = lax.rem(t, 2)
        self.other = t + 1 - 2 * self.core
        self.far = lax.rem(t + 2, 4)
        self.pairs, self.fars, self.gathers, self.mine = {}, {}, {}, {}

    def copy(self, source, target, slot, device):
        send, recv = self.sems
        c = pltpu.make_async_remote_copy(
            src_ref=source,
            dst_ref=target,
            send_sem=send.at[slot],
            recv_sem=recv.at[slot],
            device_id=(self.dp, device),
            device_id_type=MESH,
        )
        c.start()
        return c

    def share(self, ch, value):
        low, high = value[:HALF], value[HALF:]
        self.pair_out[ch] = jnp.where(self.core == 0, high, low).astype(BF16)
        self.pairs[ch] = self.copy(self.pair_out.at[ch], self.pair_in.at[ch], ch, self.other)
        self.own[ch] = jnp.where(self.core == 0, low, high)
        self.mine[ch] = lambda: self.own[ch]

    def share_held(self, ch, ref):
        self.pairs[ch] = self.copy(ref.at[1 - self.core], self.pair_in.at[ch], ch, self.other)
        self.mine[ch] = lambda: ref[self.core].astype(F32)

    def place(self, ch, parity):
        return 2 * parity + ch if ch < 2 else 2 + ch

    def swap(self, ch, parity):
        self.pairs.pop(ch).wait()
        mine = self.mine.pop(ch)() + self.pair_in[ch].astype(F32)
        self.far_out[ch] = mine.astype(BF16)
        at = self.place(ch, parity)
        self.fars[ch] = self.copy(self.far_out.at[ch], self.far_in.at[at], 4 + at, self.far)

    def total(self, ch, parity):
        self.fars.pop(ch).wait()
        return self.far_out[ch].astype(F32) + self.far_in[self.place(ch, parity)].astype(F32)

    def gather(self, key, slot, ref):
        half = ref.at[self.core]
        self.gathers[key] = self.copy(half, half, 10 + slot, self.other)

    def arrived(self, key):
        self.gathers.pop(key).wait()


class Loads:
    def __init__(self, sems):
        self.sems, self.pending, self.count = sems, {}, 0

    def start(self, key, source, target):
        c = pltpu.make_async_copy(source, target, self.sems.at[self.count])
        c.start()
        self.count += 1
        self.pending[key] = c

    def need(self, *keys):
        for key in keys:
            if key in self.pending:
                self.pending.pop(key).wait()

    def drain(self):
        self.need(*list(self.pending))


def attention_forward(n, win, wout, j, i, qkv, att, probs):
    q, k, v = (dot_nt(n, win[3 * j + c]).astype(BF16) for c in range(3))
    for c, part in enumerate((q, k, v)):
        qkv[j, c, i] = part
    key = lax.broadcasted_iota(jnp.int32, (1, PAD), 1)
    mixed = None
    for h in range(3):
        s = dot_nt(only(h, q), k) * 0.125
        s = jnp.where(key < SEQ, s, -1e30)
        e = jnp.exp(s - jnp.max(s, axis=-1, keepdims=True))
        p = e * (1.0 / jnp.sum(e, axis=-1, keepdims=True))
        p = p.astype(BF16)
        probs[j, i, h] = p
        term = dot(p, only(h, v))
        mixed = term if mixed is None else mixed + term
    mixed = mixed.astype(BF16)
    att[j, i] = mixed
    return dot(mixed, wout[j])


def attention_backward(du, win, wout, j, i, qkv, att, probs, stack):
    q, k, v = (qkv[j, c, i] for c in range(3))
    d_att = dot_nt(du, wout[j]).astype(BF16)
    dq = dk = dv = None
    for h in range(3):
        low = probs[j, i, h]
        p = low.astype(F32)
        dp = dot_nt(only(h, d_att), v)
        ds = (p * (dp - jnp.sum(p * dp, axis=-1, keepdims=True))).astype(BF16)
        terms = (dot(ds, only(h, k)), dot_tn(ds, only(h, q)), dot_tn(low, only(h, d_att)))
        dq, dk, dv = terms if dq is None else (a + b for a, b in zip((dq, dk, dv), terms))
    parts = [(dq * 0.125).astype(BF16), (dk * 0.125).astype(BF16), dv.astype(BF16)]
    stack[i * PAD : (i + 1) * PAD] = jnp.concatenate(parts + [att[j, i]], axis=1)
    return sum(dot(part, win[3 * j + c]) for c, part in enumerate(parts))


def weight_grad(g, m, left, right):
    for s in range(2):
        out = dot_tn(left[:, s * 384 : (s + 1) * 384], right).astype(BF16)
        g[m, 2 * s : 2 * s + 2] = out.reshape(2, 4, 48, D)


def head_grad(g, m, n, du, stack):
    lane = lax.broadcasted_iota(jnp.int32, (1, 256), 1)
    last = stack[:, 512:]
    zero = jnp.zeros((), BF16)
    for s in range(2):
        cut = slice(s * 384, (s + 1) * 384)
        a = dot_tn(n[:, cut], stack[:, :512]).astype(BF16)
        b = dot_tn(n[:, cut], jnp.where(lane < 64, last, zero))
        b = (b + dot_tn(du[:, cut], jnp.where(lane < 64, zero, last))).astype(BF16)
        g[m, 2 * s : 2 * s + 2, :, :, 0:512] = a.reshape(2, 4, 48, 512)
        g[m, 2 * s : 2 * s + 2, :, :, 512:] = b.reshape(2, 4, 48, 256)


class ImageSum:
    def __init__(self, spec, refs, sems, base, place, out):
        self.mats, self.width, self.order, self.ring = spec
        self.refs, self.sems, self.base, self.place, self.out = refs, sems, base, place, out
        self.copies = {}

    def send(self, name, slot, source, target, axis, k):
        y, z, x, t = self.place
        if axis == "x":
            device = grid_device(y, z, 1 - x)
        else:
            device = grid_device(y + k, z, x) if axis == "y" else grid_device(y, z + k, x)
        send, recv = self.sems
        c = pltpu.make_async_remote_copy(
            src_ref=source,
            dst_ref=target,
            send_sem=send.at[self.base + slot],
            recv_sem=recv.at[self.base + slot],
            device_id=(device, t),
            device_id_type=MESH,
        )
        c.start()
        self.copies.setdefault(name, []).append(c)

    def wait(self, name):
        for c in self.copies.pop(name, []):
            c.wait()

    def block(self, k):
        source, y, z = self.source, self.place[0], self.place[1]
        if self.order == "y":
            return source.at[:, lax.rem(y + k, 4)]
        return source.at[:, :, lax.rem(z + k, 4)]

    def start(self, source):
        self.source = source
        axis, h = self.order, self.width // 2
        r = self.refs
        low, high = pl.ds(0, h), pl.ds(h, h)
        if self.ring:
            far = self.block(2)
            self.send("a", 0, far.at[:, :, :, low], r["ra"].at[0], axis, 1)
            self.send("a", 1, far.at[:, :, :, high], r["ra"].at[1], axis, 3)
            self.send("b", 2, self.block(1).at[:, :, :, high], r["rb"].at[0, :, :, :, high], axis, 1)
            self.send("b", 3, self.block(3).at[:, :, :, low], r["rb"].at[1, :, :, :, low], axis, 3)
        else:
            for k in (2, 1, 3):
                self.send("b", k, self.block(k), r["rb"].at[k - 1], axis, k)

    def middle(self):
        r, h = self.refs, self.width // 2
        low, high = pl.ds(0, h), pl.ds(h, h)
        self.wait("a")
        for side, k, cut in ((0, 1, low), (1, 3, high)):
            near = self.block(k).at[:, :, :, cut]

            def add(m, carry, near=near, side=side):
                for b in range(4):
                    r["ra"][side, m, b] = (r["ra"][side, m, b].astype(F32) + near[m, b].astype(F32)).astype(BF16)
                return carry

            lax.fori_loop(0, self.mats, add, 0)
        self.send("b", 4, r["ra"].at[0], r["rb"].at[0, :, :, :, low], self.order, 1)
        self.send("b", 5, r["ra"].at[1], r["rb"].at[1, :, :, :, high], self.order, 3)

    def second(self):
        r = self.refs
        self.wait("b")
        own = s1 = self.block(0)

        def add(m, carry):
            for b in range(4):
                acc = own[m, b].astype(F32)
                for k in range(2 if self.ring else 3):
                    acc = acc + r["rb"][k, m, b].astype(F32)
                s1[m, b] = acc.astype(BF16)
            return carry

        lax.fori_loop(0, self.mats, add, 0)
        axis = "z" if self.order == "y" else "y"
        mine = self.place[1] if axis == "z" else self.place[0]
        for k in (2, 1, 3):
            self.send("c", 5 + k, s1.at[:, lax.rem(mine + k, 4)], r["rc"].at[k - 1], axis, k)

    def total(self, m):
        r = self.refs
        y, z, x, t = self.place
        acc = self.block(0)[m, z if self.order == "y" else y].astype(F32)
        for k in range(3):
            acc = acc + r["rc"][k, m].astype(F32)
        return acc

    def third(self):
        r = self.refs
        x = self.place[2]
        self.wait("c")
        for m in range(0, self.mats, 2):
            pieces = [self.total(n) for n in (m, min(m + 1, self.mats - 1))]
            pieces = [jnp.where(x == 0, v[24:], v[:24]) for v in pieces]
            r["xs"][m // 2] = jnp.concatenate(pieces, axis=0).astype(BF16)
        self.send("d", 9, r["xs"], r["xr"], "x", 0)

    def finish(self):
        r = self.refs
        x = self.place[2]
        self.wait("d")
        for m in range(self.mats):
            theirs = r["xr"][m // 2].astype(F32)
            v = self.total(m)
            mine = jnp.where(x == 0, v[:24], v[24:])
            self.out(m, mine + theirs[24 * (m % 2) : 24 * (m % 2) + 24])


GROUPS = {
    "eay": (2, 768, "y", True),
    "eaz": (2, 768, "z", True),
    "eby": (2, 768, "y", True),
    "ebz": (2, 768, "z", True),
    "m0": (1, 768, "y", True),
    "m1": (1, 768, "z", True),
    "a1y": (1, 384, "y", False),
    "a1z": (1, 384, "z", False),
    "a0y": (1, 384, "y", False),
    "a0z": (1, 384, "z", False),
    "n": (1, 128, "y", False),
}


def group_scratch(spec):
    mats, width, order, ring = spec
    pairs = (mats + 1) // 2
    shapes = {
        "rb": pltpu.VMEM((2 if ring else 3, mats, 4, 48, width), BF16),
        "rc": pltpu.VMEM((3, mats, 48, width), BF16),
        "xs": pltpu.VMEM((pairs, 48, width), BF16),
        "xr": pltpu.VMEM((pairs, 48, width), BF16),
    }
    if ring:
        shapes["ra"] = pltpu.VMEM((2, mats, 4, 48, width // 2), BF16)
    return shapes


def layers_kernel(
    tokens, cot, routes, slots, gates, gain, bias, win, wout, m1_h, m2_h, ein, eout, *refs
):
    (
        out_o, token_o, gain_o, bias_o, heads_in_o, heads_out_o, m_in_o, m_out_o, e_in_o, e_out_o,
    ) = refs[:10]
    (
        n0, n1, n2, n3, du2, du1, du0, qkv, att, probs, act, dgelu, streams, g2,
        pick, spread, gate, buf, drow, weighted, dbuf, m1, m2, g, ge, gn, sums, sums_in,
        own, pair_out, pair_in, far_out, far_in,
        send, recv, group_send, group_recv, load_sem,
    ) = refs[10:48]
    rest = refs[48:]
    dn, mo, cotp = n3, du0, du1
    stack = weighted.at[0 : 2 * PAD]
    dhid = dbuf
    links = TensorLinks((own, pair_out, pair_in, far_out, far_in), (send, recv))
    core = links.core
    dp = links.dp
    t = lax.axis_index("tensor")
    y, z, x = dp // 8, lax.rem(dp // 2, 4), lax.rem(dp, 2)
    place = (y, z, x, t)

    barrier = pltpu.get_barrier_semaphore()
    for device in ((dp, links.other), (dp, links.far), (grid_device(y, z, 1 - x), t)):
        pl.semaphore_signal(barrier, inc=1, device_id=device, device_id_type=MESH)
    for k in (1, 2, 3):
        for device in (grid_device(y + k, z, x), grid_device(y, z + k, x)):
            pl.semaphore_signal(barrier, inc=1, device_id=(device, t), device_id_type=MESH)

    def store(ref, *index):
        def put(m, value):
            ref[index] = value

        return put

    def store_expert(ref, base):
        def put(m, value):
            ref[base + m] = value

        return put

    def store_heads(j, first):
        def put(m, value):
            width = heads_in_o.shape[-1]
            low, high = value[:, :width], pltpu.roll(value, width, 1)[:, :width]
            if first == 0:
                heads_in_o[j, 0] = low
                heads_in_o[j, 1] = high
            else:
                heads_in_o[j, 2] = low
                heads_out_o[j] = high

        return put

    def store_norms(m, value):
        turned = jnp.concatenate([value, jnp.zeros((104, 128), F32)], axis=0).T
        gain_o[...] = turned[0:4, :24]
        bias_o[...] = turned[4:8, :24]

    outs = {
        "eay": store_expert(e_in_o, 0),
        "eaz": store_expert(e_out_o, 0),
        "eby": store_expert(e_in_o, 2),
        "ebz": store_expert(e_out_o, 2),
        "m0": store(m_in_o, Ellipsis),
        "m1": store(m_out_o, Ellipsis),
        "a1y": store_heads(1, 0),
        "a1z": store_heads(1, 384),
        "a0y": store_heads(0, 0),
        "a0z": store_heads(0, 384),
        "n": store_norms,
    }
    groups = {}
    for at, (name, spec) in enumerate(GROUPS.items()):
        keys = list(group_scratch(spec))
        held = dict(zip(keys, rest[: len(keys)]))
        rest = rest[len(keys) :]
        groups[name] = ImageSum(spec, held, (group_send, group_recv), 10 * at, place, outs[name])

    loads = Loads(load_sem)
    loads.start("m1", m1_h, m1)
    loads.start("m2", m2_h, m2)

    def fetch(e):
        loads.start(("in", e), ein.at[e], g.at[2 * (e % 2)])
        loads.start(("out", e), eout.at[e], g.at[2 * (e % 2) + 1])

    fetch(0)
    fetch(1)
    rows_of = tokens.shape[0]

    def placement():
        row = lax.broadcasted_iota(jnp.int32, (2 * PAD, rows_of), 0)
        column = lax.broadcasted_iota(jnp.int32, (2 * PAD, rows_of), 1)
        image = (row >= PAD).astype(jnp.int32)
        inside = row - image * PAD < SEQ
        hit = jnp.logical_and(inside, column == row - image * (PAD - SEQ))
        return jnp.where(hit, 1.0, 0.0).astype(BF16)

    def padded(ref):
        return dot(placement(), ref[...]).astype(BF16).reshape(2, 2, HALF, D)

    def norm_rows(s, v):
        return (normalize(v)[0] * gain[s : s + 1] + bias[s : s + 1]).astype(BF16)

    mo[...] = padded(tokens)
    for i in range(2):
        for half in range(2):
            n0[i, half] = norm_rows(0, mo[i, half].astype(F32))
        streams[0, i] = mo[i, core].astype(F32)

    def rows(ref, i):
        return ref[i].reshape(PAD, D)

    def block(s, i):
        if s != 1:
            return attention_forward(rows((n0, None, n2)[s], i), win, wout, s // 2, i, qkv, att, probs)
        loads.need("m1", "m2")
        hidden = dot(rows(n1, i), m1[...])
        act[i], dgelu[i] = gelu_pair(hidden)
        return dot(act[i], m2[...])

    normed = (n0, n1, n2, n3)

    def finish_forward(s, i):
        v = streams[s, i] + links.total(i, s % 2)
        streams[s + 1, i] = v
        normed[s + 1][i, core] = norm_rows(s + 1, v)
        links.gather((s, i), 2 * s + i, normed[s + 1].at[i])

    def hits():
        kept_choice = slots[...] < CAPACITY
        index = jnp.where(kept_choice, routes[...] * SLOTS + slots[...], -1)
        number = lax.broadcasted_iota(jnp.int32, (EXPERTS * SLOTS, rows_of), 0)
        return [number == index[k : k + 1] for k in range(2)]

    def make_pick():
        first, second = hits()
        flat = jnp.where(jnp.logical_or(first, second), 1.0, 0.0).astype(BF16)
        pick[...] = dot_nt(flat, placement()).astype(BF16)

    def make_spread():
        first, second = hits()
        flat = jnp.where(jnp.logical_or(first, second), 1.0, 0.0).astype(BF16)
        spread[...] = dot_nt(placement(), flat).astype(BF16)

    def make_gate():
        gate[...] = sum(
            jnp.sum(jnp.where(hit, gates[k : k + 1], 0.0), axis=1, keepdims=True)
            for k, hit in enumerate(hits())
        )

    def make_cot():
        cotp[...] = padded(cot)

    def make_drow():
        drow[...] = (dot(pick[...], cotp[...].reshape(2 * PAD, D)) * gate[...]).astype(BF16)

    fill = (make_pick, make_spread, make_gate, make_cot, make_drow, None)
    steps = [(s, i) for s in range(3) for i in range(2)]
    for at, (s, i) in enumerate(steps):
        if s > 0:
            links.arrived((s - 1, i))
        term = block(s, i)
        if at == 0:
            pl.semaphore_wait(barrier, 9)
        links.share(i, term)
        if fill[at] is not None:
            fill[at]()
        links.swap(i, s % 2)
        if at > 0:
            finish_forward(*steps[at - 1])
    finish_forward(*steps[-1])

    for i in range(2):
        links.arrived((2, i))
    buf[...] = dot(pick[...], n3[...].reshape(2 * PAD, D)).astype(BF16)
    for e in range(EXPERTS):
        cut = pl.ds(e * SLOTS, SLOTS)
        loads.need(("in", e), ("out", e))
        w_in = g[2 * (e % 2)].reshape(D, D)
        w_out = g[2 * (e % 2) + 1].reshape(D, D)
        a, slope = gelu_pair(dot(buf[cut], w_in))
        d = (slope * dot_nt(drow[cut], w_out)).astype(BF16)
        weighted[cut] = (dot(a, w_out) * gate[cut]).astype(BF16)
        dbuf[cut] = dot_nt(d, w_in).astype(BF16)
        weight_grad(ge, e, buf[cut], d)
        weight_grad(ge, EXPERTS + e, drow[cut], a)
        if e + 2 < EXPERTS:
            fetch(e + 2)
        if e == 1:
            groups["eay"].start(ge.at[0:2])
            groups["eaz"].start(ge.at[4:6])
        if e == 3:
            groups["eby"].start(ge.at[2:4])
            groups["ebz"].start(ge.at[6:8])
    dn[...] = dot(spread[...], dbuf[...]).astype(BF16).reshape(2, 2, HALF, D)
    for i in range(2):
        links.share_held(i, dn.at[i])
    mo[...] = dot(spread[...], weighted[...]).astype(BF16).reshape(2, 2, HALF, D)

    def flat(ref):
        return ref[...].reshape(2 * PAD, D)

    def share(parity, i, value):
        links.share(i, value)
        links.swap(i, parity)

    def finish(s, parity, i, base, target, slot):
        dv, gain_term, bias_term = norm_back(streams[s, i], gain[s : s + 1], links.total(i, parity))
        sums[s : s + 1] = sums[s : s + 1] + gain_term
        sums[4 + s : 5 + s] = sums[4 + s : 5 + s] + bias_term
        v = base[i].astype(F32) + dv if s < 3 else base[i, core].astype(F32) + dv
        if s > 0:
            g2[i] = v
            target[i, core] = v.astype(BF16)
        else:
            target[i, core] = v
        links.gather((s, i), 2 * slot + i, target.at[i])

    sums[...] = jnp.zeros_like(sums)
    for i in range(2):
        links.swap(i, 1)
    for i in range(2):
        links.share_held(2 + i, mo.at[i])
    for i in range(2):
        finish(3, 1, i, cotp, du2, 0)
    for i in range(2):
        links.swap(2 + i, 0)

    for i in range(2):
        links.arrived((3, i))
        share(0, i, attention_backward(rows(du2, i), win, wout, 1, i, qkv, att, probs, stack))
    for name in ("eay", "eaz"):
        groups[name].middle()
    head_grad(g, 3, flat(n2), flat(du2), stack)
    groups["a1y"].start(g.at[3:4, :, :, :, 0:384])
    groups["a1z"].start(g.at[3:4, :, :, :, 384:768])
    for i in range(2):
        finish(2, 0, i, g2, du1, 1)
    for i in range(2):
        out_o[i, core] = streams[3, i] + links.total(2 + i, 0)
        links.gather((4, i), 8 + i, out_o.at[i])

    for i in range(2):
        links.arrived((2, i))
        d = (dgelu[i] * dot_nt(rows(du1, i), m2[...])).astype(BF16)
        dhid[pl.ds(i * PAD, PAD)] = d
        share(1, i, dot_nt(d, m1[...]))
    for name in ("eby", "ebz"):
        groups[name].middle()
    weight_grad(g, 0, flat(n1), dhid[0 : 2 * PAD])
    groups["m0"].start(g.at[0:1])
    weight_grad(g, 1, flat(du1), act[...].reshape(2 * PAD, D))
    groups["m1"].start(g.at[1:2])
    for i in range(2):
        finish(1, 1, i, g2, du0, 2)

    for i in range(2):
        links.arrived((1, i))
        share(0, i, attention_backward(rows(du0, i), win, wout, 0, i, qkv, att, probs, stack))
    for name in ("eay", "eaz"):
        groups[name].second()
    head_grad(g, 2, flat(n0), flat(du0), stack)
    groups["a0y"].start(g.at[2:3, :, :, :, 0:384])
    groups["a0z"].start(g.at[2:3, :, :, :, 384:768])
    for i in range(2):
        finish(0, 0, i, g2, token_o, 3)
    both = links.copy(sums, sums_in, 20, links.other)
    for name in ("m0", "m1"):
        groups[name].middle()
    for name in ("a1y", "a1z", "eby", "ebz"):
        groups[name].second()
    both.wait()
    wide = jnp.concatenate([sums[...] + sums_in[...], jnp.zeros((120, D), F32)], axis=0)
    gn[0] = wide.T.astype(BF16).reshape(4, 4, 48, 128)
    groups["n"].start(gn)
    for name in ("eay", "eaz"):
        groups[name].third()
    for name in ("a0y", "a0z", "m0", "m1", "n"):
        groups[name].second()
    last = ("a1y", "a1z", "eby", "ebz", "a0y", "a0z", "m0", "m1", "n")
    for name in last:
        groups[name].third()
    for name in ("eay", "eaz") + last:
        groups[name].finish()
    for i in range(2):
        links.arrived((0, i))
        links.arrived((4, i))


def publish_kernel(*refs):
    count = (len(refs) - 3) // 2
    pads, sems = refs[-3:-1], refs[-1]
    targets = list(pads) + list(refs[count + 2 : 2 * count])
    copies = [pltpu.make_async_copy(refs[k], targets[k], sems.at[k]) for k in range(count)]
    for copy in copies:
        copy.start()
    for k in range(2):
        copies[k].wait()
        for i in range(2):
            refs[count + k][i * SEQ : (i + 1) * SEQ] = pads[k][i].reshape(PAD, D)[:SEQ]
    for copy in copies[2:]:
        copy.wait()


def link_scratch(channels, sems):
    return [
        pltpu.VMEM((2, HALF, D), F32),
        pltpu.VMEM((2, HALF, D), BF16),
        pltpu.VMEM((channels, HALF, D), BF16),
        pltpu.VMEM((channels, HALF, D), BF16),
        pltpu.VMEM((2 + channels, HALF, D), BF16),
        pltpu.SemaphoreType.DMA((sems,)),
        pltpu.SemaphoreType.DMA((sems,)),
    ]


def local(
    tokens,
    norm_gain,
    norm_bias,
    attn_in,
    attn_out,
    mlp_in,
    mlp_out,
    expert_in,
    expert_out,
    routes,
    slot_index,
    gate_weights,
    cotangent,
):
    head_width = attn_out.shape[1]
    slots = EXPERTS * SLOTS
    rows = tokens.shape[0]
    whole = pl.BlockSpec(memory_space=pltpu.VMEM)
    hbm = pl.BlockSpec(memory_space=pl.ANY)
    shape = jax.ShapeDtypeStruct
    half_rows = (2, 2, HALF, D)
    win = jnp.swapaxes(attn_in, 2, 3).reshape(6, head_width, D)
    scratch = (
        [pltpu.VMEM(half_rows, BF16)] * 7
        + [
            pltpu.VMEM((2, 3, 2, PAD, head_width), BF16),
            pltpu.VMEM((2, 2, PAD, head_width), BF16),
            pltpu.VMEM((2, 2, 3, PAD, PAD), BF16),
            pltpu.VMEM((2, PAD, D), BF16),
            pltpu.VMEM((2, PAD, D), F32),
            pltpu.VMEM((4, 2, HALF, D), F32),
            pltpu.VMEM((2, HALF, D), F32),
            pltpu.VMEM((slots, 2 * PAD), BF16),
            pltpu.VMEM((2 * PAD, slots), BF16),
            pltpu.VMEM((slots, 1), F32),
        ]
        + [pltpu.VMEM((slots, D), BF16)] * 4
        + [
            pltpu.VMEM((D, D), BF16),
            pltpu.VMEM((D, D), BF16),
            pltpu.VMEM((4, 4, 4, 48, D), BF16),
            pltpu.VMEM((2 * EXPERTS, 4, 4, 48, D), BF16),
            pltpu.VMEM((1, 4, 4, 48, 128), BF16),
            pltpu.VMEM((8, D), F32),
            pltpu.VMEM((8, D), F32),
        ]
        + link_scratch(4, 22)
        + [
            pltpu.SemaphoreType.DMA((10 * len(GROUPS),)),
            pltpu.SemaphoreType.DMA((10 * len(GROUPS),)),
            pltpu.SemaphoreType.DMA((10,)),
        ]
    )
    for spec in GROUPS.values():
        scratch += list(group_scratch(spec).values())
    results = pl.pallas_call(
        layers_kernel,
        out_shape=[
            shape(half_rows, F32),
            shape(half_rows, F32),
            shape((4, 24), F32),
            shape((4, 24), F32),
            shape((2, 3, 24, head_width), F32),
            shape((2, 24, head_width), F32),
            shape((24, D), F32),
            shape((24, D), F32),
            shape((EXPERTS, 24, D), F32),
            shape((EXPERTS, 24, D), F32),
        ],
        in_specs=[whole] * 9 + [hbm] * 4,
        out_specs=[whole] * 10,
        scratch_shapes=scratch,
        compiler_params=pltpu.CompilerParams(
            collective_id=1, has_side_effects=True, vmem_limit_bytes=63 << 20
        ),
        name="layers",
    )(
        tokens, cotangent, routes.T, slot_index.T, gate_weights.T, norm_gain, norm_bias, win, attn_out,
        mlp_in, mlp_out, expert_in.reshape(EXPERTS, 4, 4, 48, D), expert_out.reshape(EXPERTS, 4, 4, 48, D),
    )
    out, token_grad, gains, biases, heads_in, heads_out, m_in, m_out, e_in, e_out = pl.pallas_call(
        publish_kernel,
        out_shape=[shape((rows, D), F32)] * 2 + [shape(r.shape, r.dtype) for r in results[2:]],
        in_specs=[hbm] * len(results),
        out_specs=[whole] * len(results),
        scratch_shapes=[pltpu.VMEM(half_rows, F32)] * 2 + [pltpu.SemaphoreType.DMA((len(results),))],
        name="publish",
    )(*results)
    return (
        out,
        token_grad,
        gains,
        biases,
        heads_in,
        jnp.swapaxes(heads_out, 1, 2),
        m_in,
        m_out.T,
        e_in,
        jnp.swapaxes(e_out, 1, 2),
    )


def solution(mesh):
    placed = (
        P("dp", None),
        P(),
        P(),
        P(None, None, None, "tensor"),
        P(None, "tensor", None),
        P(None, "tensor"),
        P("tensor", None),
        P(None, None, "tensor"),
        P(None, "tensor", None),
        P("dp", None),
        P("dp", None),
        P("dp", None),
        P("dp", None),
    )
    return jax.shard_map(
        local,
        mesh=mesh,
        in_specs=placed,
        out_specs=(
            P("dp", None),
            P("dp", None),
            P(None, "dp"),
            P(None, "dp"),
            P(None, None, "dp", "tensor"),
            P(None, "tensor", "dp"),
            P("dp", "tensor"),
            P("tensor", "dp"),
            P(None, "dp", "tensor"),
            P(None, "tensor", "dp"),
        ),
        check_vma=False,
    )
```

```python
import functools

import jax
import jax.numpy as jnp
from jax import lax
from jax.experimental import pallas as pl
from jax.experimental.pallas import tpu as pltpu
from jax.sharding import PartitionSpec as P

D = 768
HEAD_DIM = 64
SEQ = 197
HALF = 112
PAD = 2 * HALF
CAPACITY = 168
SLOTS = 176
EXPERTS = 4
NORM_EPSILON = 1e-06
MESH = pl.DeviceIdType.MESH
F32 = jnp.float32
BF16 = jnp.bfloat16


def dot(a, b):
    return lax.dot_general(a, b, (((1,), (0,)), ((), ())), preferred_element_type=F32)


def dot_nt(a, b):
    return lax.dot_general(a, b, (((1,), (1,)), ((), ())), preferred_element_type=F32)


def dot_tn(a, b):
    return lax.dot_general(a, b, (((0,), (0,)), ((), ())), preferred_element_type=F32)


def grid_device(y, z, x):
    return (lax.rem(y + 8, 4) * 4 + lax.rem(z + 8, 4)) * 2 + x


def normalize(v):
    center = v - jnp.mean(v, axis=-1, keepdims=True)
    spread = jnp.mean(center * center, axis=-1, keepdims=True)
    scale = lax.rsqrt(spread + NORM_EPSILON)
    return center * scale, scale


def norm_back(v, gain_row, upstream):
    nhat, scale = normalize(v)
    scaled = upstream * gain_row
    mean = jnp.mean(scaled, axis=-1, keepdims=True)
    along = jnp.mean(scaled * nhat, axis=-1, keepdims=True)
    dv = (scaled - mean - nhat * along) * scale
    gain_term = jnp.sum(upstream * nhat, axis=0, keepdims=True)
    bias_term = jnp.sum(upstream, axis=0, keepdims=True)
    return dv, gain_term, bias_term


def gelu_share(h):
    return 0.5 * (1.0 + lax.erf(h * 0.7071067811865476))


def gelu_slope(h, phi):
    return phi + h * (jnp.exp(-0.5 * h * h) * 0.3989422804014327)


def gelu_pair(h):
    phi = gelu_share(h)
    return (h * phi).astype(BF16), gelu_slope(h, phi)


def head_mask(h, width):
    lane = lax.broadcasted_iota(jnp.int32, (1, width), 1)
    return jnp.logical_and(lane >= h * HEAD_DIM, lane < (h + 1) * HEAD_DIM)


def only(h, v):
    return jnp.where(head_mask(h, v.shape[1]), v, jnp.zeros((), v.dtype))


class TensorLinks:
    def __init__(self, refs, sems):
        self.own, self.pair_out, self.pair_in, self.far_out, self.far_in = refs
        self.sems = sems
        self.dp = lax.axis_index("dp")
        t = lax.axis_index("tensor")
        self.core = lax.rem(t, 2)
        self.other = t + 1 - 2 * self.core
        self.far = lax.rem(t + 2, 4)
        self.pairs, self.fars, self.gathers, self.mine = {}, {}, {}, {}

    def copy(self, source, target, slot, device):
        send, recv = self.sems
        c = pltpu.make_async_remote_copy(
            src_ref=source,
            dst_ref=target,
            send_sem=send.at[slot],
            recv_sem=recv.at[slot],
            device_id=(self.dp, device),
            device_id_type=MESH,
        )
        c.start()
        return c

    def share(self, ch, value):
        low, high = value[:HALF], value[HALF:]
        self.pair_out[ch] = jnp.where(self.core == 0, high, low).astype(BF16)
        self.pairs[ch] = self.copy(self.pair_out.at[ch], self.pair_in.at[ch], ch, self.other)
        self.own[ch] = jnp.where(self.core == 0, low, high)
        self.mine[ch] = lambda: self.own[ch]

    def share_held(self, ch, ref):
        self.pairs[ch] = self.copy(ref.at[1 - self.core], self.pair_in.at[ch], ch, self.other)
        self.mine[ch] = lambda: ref[self.core].astype(F32)

    def place(self, ch, parity):
        return 2 * parity + ch if ch < 2 else 2 + ch

    def swap(self, ch, parity):
        self.pairs.pop(ch).wait()
        mine = self.mine.pop(ch)() + self.pair_in[ch].astype(F32)
        self.far_out[ch] = mine.astype(BF16)
        at = self.place(ch, parity)
        self.fars[ch] = self.copy(self.far_out.at[ch], self.far_in.at[at], 4 + at, self.far)

    def total(self, ch, parity):
        self.fars.pop(ch).wait()
        return self.far_out[ch].astype(F32) + self.far_in[self.place(ch, parity)].astype(F32)

    def gather(self, key, slot, ref):
        half = ref.at[self.core]
        self.gathers[key] = self.copy(half, half, 10 + slot, self.other)

    def arrived(self, key):
        self.gathers.pop(key).wait()


class Loads:
    def __init__(self, sems):
        self.sems, self.pending, self.count = sems, {}, 0

    def start(self, key, source, target):
        c = pltpu.make_async_copy(source, target, self.sems.at[self.count])
        c.start()
        self.count += 1
        self.pending[key] = c

    def need(self, *keys):
        for key in keys:
            if key in self.pending:
                self.pending.pop(key).wait()

    def drain(self):
        self.need(*list(self.pending))


def attention_forward(n, win, wout, j, i, qkv, att, probs):
    q, k, v = (dot_nt(n, win[3 * j + c]).astype(BF16) for c in range(3))
    for c, part in enumerate((q, k, v)):
        qkv[j, c, i] = part
    key = lax.broadcasted_iota(jnp.int32, (1, PAD), 1)
    mixed = None
    for h in range(3):
        s = dot_nt(only(h, q), k) * 0.125
        s = jnp.where(key < SEQ, s, -1e30)
        e = jnp.exp(s - jnp.max(s, axis=-1, keepdims=True))
        p = e * (1.0 / jnp.sum(e, axis=-1, keepdims=True))
        p = p.astype(BF16)
        probs[j, i, h] = p
        term = dot(p, only(h, v))
        mixed = term if mixed is None else mixed + term
    mixed = mixed.astype(BF16)
    att[j, i] = mixed
    return dot(mixed, wout[j])


def attention_backward(du, win, wout, j, i, qkv, att, probs, stack):
    q, k, v = (qkv[j, c, i] for c in range(3))
    d_att = dot_nt(du, wout[j]).astype(BF16)
    dq = dk = dv = None
    for h in range(3):
        low = probs[j, i, h]
        p = low.astype(F32)
        dp = dot_nt(only(h, d_att), v)
        ds = (p * (dp - jnp.sum(p * dp, axis=-1, keepdims=True))).astype(BF16)
        terms = (dot(ds, only(h, k)), dot_tn(ds, only(h, q)), dot_tn(low, only(h, d_att)))
        dq, dk, dv = terms if dq is None else (a + b for a, b in zip((dq, dk, dv), terms))
    parts = [(dq * 0.125).astype(BF16), (dk * 0.125).astype(BF16), dv.astype(BF16)]
    stack[i * PAD : (i + 1) * PAD] = jnp.concatenate(parts + [att[j, i]], axis=1)
    return sum(dot(part, win[3 * j + c]) for c, part in enumerate(parts))


def weight_grad(g, m, left, right):
    for s in range(2):
        out = dot_tn(left[:, s * 384 : (s + 1) * 384], right).astype(BF16)
        g[m, 2 * s : 2 * s + 2] = out.reshape(2, 4, 48, D)


def head_grad(g, m, n, du, stack):
    lane = lax.broadcasted_iota(jnp.int32, (1, 256), 1)
    last = stack[:, 512:]
    zero = jnp.zeros((), BF16)
    for s in range(2):
        cut = slice(s * 384, (s + 1) * 384)
        a = dot_tn(n[:, cut], stack[:, :512]).astype(BF16)
        b = dot_tn(n[:, cut], jnp.where(lane < 64, last, zero))
        b = (b + dot_tn(du[:, cut], jnp.where(lane < 64, zero, last))).astype(BF16)
        g[m, 2 * s : 2 * s + 2, :, :, 0:512] = a.reshape(2, 4, 48, 512)
        g[m, 2 * s : 2 * s + 2, :, :, 512:] = b.reshape(2, 4, 48, 256)


class ImageSum:
    def __init__(self, spec, refs, sems, base, place, out):
        self.mats, self.width, self.order, self.ring = spec
        self.refs, self.sems, self.base, self.place, self.out = refs, sems, base, place, out
        self.copies = {}

    def send(self, name, slot, source, target, axis, k):
        y, z, x, t = self.place
        if axis == "x":
            device = grid_device(y, z, 1 - x)
        else:
            device = grid_device(y + k, z, x) if axis == "y" else grid_device(y, z + k, x)
        send, recv = self.sems
        c = pltpu.make_async_remote_copy(
            src_ref=source,
            dst_ref=target,
            send_sem=send.at[self.base + slot],
            recv_sem=recv.at[self.base + slot],
            device_id=(device, t),
            device_id_type=MESH,
        )
        c.start()
        self.copies.setdefault(name, []).append(c)

    def wait(self, name):
        for c in self.copies.pop(name, []):
            c.wait()

    def block(self, k):
        source, y, z = self.source, self.place[0], self.place[1]
        if self.order == "y":
            return source.at[:, lax.rem(y + k, 4)]
        return source.at[:, :, lax.rem(z + k, 4)]

    def start(self, source):
        self.source = source
        axis = self.order
        r = self.refs
        low, high = pl.ds(0, 2), pl.ds(2, 2)
        if self.ring:
            far = self.block(2)
            self.send("a", 0, far.at[:, low], r["ra"].at[0], axis, 1)
            self.send("a", 1, far.at[:, high], r["ra"].at[1], axis, 3)
            self.send("b", 2, self.block(1).at[:, high], r["rb"].at[0, :, high], axis, 1)
            self.send("b", 3, self.block(3).at[:, low], r["rb"].at[1, :, low], axis, 3)
        else:
            for k in (2, 1, 3):
                self.send("b", k, self.block(k), r["rb"].at[k - 1], axis, k)

    def middle(self):
        r = self.refs
        low, high = pl.ds(0, 2), pl.ds(2, 2)
        self.wait("a")
        for side, k, cut in ((0, 1, low), (1, 3, high)):
            near = self.block(k).at[:, cut]

            def add(m, carry, near=near, side=side):
                for b in range(2):
                    r["ra"][side, m, b] = (r["ra"][side, m, b].astype(F32) + near[m, b].astype(F32)).astype(BF16)
                return carry

            lax.fori_loop(0, self.mats, add, 0)
        self.send("b", 4, r["ra"].at[0], r["rb"].at[0, :, low], self.order, 1)
        self.send("b", 5, r["ra"].at[1], r["rb"].at[1, :, high], self.order, 3)

    def second(self):
        r = self.refs
        self.wait("b")
        own = s1 = self.block(0)

        def add(m, carry):
            for b in range(4):
                acc = own[m, b].astype(F32)
                for k in range(2 if self.ring else 3):
                    acc = acc + r["rb"][k, m, b].astype(F32)
                s1[m, b] = acc.astype(BF16)
            return carry

        lax.fori_loop(0, self.mats, add, 0)
        axis = "z" if self.order == "y" else "y"
        mine = self.place[1] if axis == "z" else self.place[0]
        if self.mats == 2:
            h = self.width // 2
            low, high = pl.ds(0, h), pl.ds(h, h)
            right, far, left = (s1.at[:, lax.rem(mine + k, 4)] for k in (1, 2, 3))
            self.send("e", 6, far.at[:, :, low], r["rc"].at[0, :, :, low], axis, 1)
            self.send("e", 7, far.at[:, :, high], r["rc"].at[0, :, :, high], axis, 3)
            self.send("c", 8, right.at[:, :, high], r["rc"].at[1, :, :, high], axis, 1)
            self.send("c", 9, left.at[:, :, low], r["rc"].at[2, :, :, low], axis, 3)
            return
        for k in (2, 1, 3):
            self.send("c", 5 + k, s1.at[:, lax.rem(mine + k, 4)], r["rc"].at[k - 1], axis, k)

    def relay(self):
        r, h = self.refs, self.width // 2
        axis = "z" if self.order == "y" else "y"
        mine = self.place[1] if axis == "z" else self.place[0]
        low, high = pl.ds(0, h), pl.ds(h, h)
        s1 = self.block(0)
        right, left = lax.rem(mine + 1, 4), lax.rem(mine + 3, 4)
        self.wait("e")
        for m in range(self.mats):
            for near, cut in ((right, low), (left, high)):
                acc = r["rc"][0, m, :, cut].astype(F32) + s1[m, near, :, cut].astype(F32)
                r["rc"][0, m, :, cut] = acc.astype(BF16)
        self.send("c", 10, r["rc"].at[0, :, :, low], r["rc"].at[1, :, :, low], axis, 1)
        self.send("c", 11, r["rc"].at[0, :, :, high], r["rc"].at[2, :, :, high], axis, 3)

    def total(self, m):
        r = self.refs
        y, z, x, t = self.place
        acc = self.block(0)[m, z if self.order == "y" else y].astype(F32)
        for k in range(1 if self.mats == 2 else 0, 3):
            acc = acc + r["rc"][k, m].astype(F32)
        return acc

    def third(self):
        r = self.refs
        x = self.place[2]
        self.wait("c")
        for m in range(0, self.mats, 2):
            pieces = [self.total(n) for n in (m, min(m + 1, self.mats - 1))]
            pieces = [jnp.where(x == 0, v[24:], v[:24]) for v in pieces]
            r["xs"][m // 2] = jnp.concatenate(pieces, axis=0).astype(BF16)
        self.send("d", 12, r["xs"], r["xr"], "x", 0)

    def finish(self):
        r = self.refs
        x = self.place[2]
        self.wait("d")
        for m in range(self.mats):
            theirs = r["xr"][m // 2].astype(F32)
            v = self.total(m)
            mine = jnp.where(x == 0, v[:24], v[24:])
            self.out(m, mine + theirs[24 * (m % 2) : 24 * (m % 2) + 24])


GROUPS = {
    "eay": (2, 768, "y", True),
    "eaz": (2, 768, "z", True),
    "eby": (2, 768, "y", True),
    "ebz": (2, 768, "z", True),
    "m0": (1, 768, "y", True),
    "m1": (1, 768, "z", True),
    "a1y": (1, 384, "y", True),
    "a1z": (1, 384, "z", True),
    "a0y": (1, 384, "y", False),
    "a0z": (1, 384, "z", False),
    "n": (1, 128, "y", False),
}


def group_scratch(spec):
    mats, width, order, ring = spec
    pairs = (mats + 1) // 2
    shapes = {
        "rb": pltpu.VMEM((2 if ring else 3, mats, 4, 48, width), BF16),
        "rc": pltpu.VMEM((3, mats, 48, width), BF16),
        "xs": pltpu.VMEM((pairs, 48, width), BF16),
        "xr": pltpu.VMEM((pairs, 48, width), BF16),
    }
    if ring:
        shapes["ra"] = pltpu.VMEM((2, mats, 2, 48, width), BF16)
    return shapes


def layers_kernel(
    tokens, cot, routes, slots, gates, gain, bias, win_h, wout_h, m1_h, m2_h, ein, eout, *refs
):
    (
        out_o, token_o, gain_o, bias_o, heads_in_o, heads_out_o, m_in_o, m_out_o, e_in_o, e_out_o,
    ) = refs[:10]
    (
        n0, n1, n2, n3, du2, du1, du0, qkv, att, probs, act, dgelu, streams, g2,
        pick, spread, gate, buf, drow, weighted, dbuf, win, wout, m1, m2, g, ge, gn, sums, sums_in,
        own, pair_out, pair_in, far_out, far_in,
        send, recv, group_send, group_recv, load_sem,
    ) = refs[10:50]
    rest = refs[50:]
    mo, cotp = du0, du1
    stack = weighted.at[0 : 2 * PAD]
    dhid = dbuf
    links = TensorLinks((own, pair_out, pair_in, far_out, far_in), (send, recv))
    core = links.core
    dp = links.dp
    t = lax.axis_index("tensor")
    y, z, x = dp // 8, lax.rem(dp // 2, 4), lax.rem(dp, 2)
    place = (y, z, x, t)

    barrier = pltpu.get_barrier_semaphore()
    for device in ((dp, links.other), (dp, links.far), (grid_device(y, z, 1 - x), t)):
        pl.semaphore_signal(barrier, inc=1, device_id=device, device_id_type=MESH)
    for k in (1, 2, 3):
        for device in (grid_device(y + k, z, x), grid_device(y, z + k, x)):
            pl.semaphore_signal(barrier, inc=1, device_id=(device, t), device_id_type=MESH)

    def store(ref, *index):
        def put(m, value):
            ref[index] = value

        return put

    def store_expert(ref, base):
        def put(m, value):
            ref[base + m] = value

        return put

    def store_heads(j, first):
        def put(m, value):
            width = heads_in_o.shape[-1]
            low, high = value[:, :width], pltpu.roll(value, width, 1)[:, :width]
            if first == 0:
                heads_in_o[j, 0] = low
                heads_in_o[j, 1] = high
            else:
                heads_in_o[j, 2] = low
                heads_out_o[j] = high

        return put

    def store_norms(m, value):
        turned = jnp.concatenate([value, jnp.zeros((104, 128), F32)], axis=0).T
        gain_o[...] = turned[0:4, :24]
        bias_o[...] = turned[4:8, :24]

    outs = {
        "eay": store_expert(e_in_o, 0),
        "eaz": store_expert(e_out_o, 0),
        "eby": store_expert(e_in_o, 2),
        "ebz": store_expert(e_out_o, 2),
        "m0": store(m_in_o, Ellipsis),
        "m1": store(m_out_o, Ellipsis),
        "a1y": store_heads(1, 0),
        "a1z": store_heads(1, 384),
        "a0y": store_heads(0, 0),
        "a0z": store_heads(0, 384),
        "n": store_norms,
    }
    groups = {}
    for at, (name, spec) in enumerate(GROUPS.items()):
        keys = list(group_scratch(spec))
        held = dict(zip(keys, rest[: len(keys)]))
        rest = rest[len(keys) :]
        groups[name] = ImageSum(spec, held, (group_send, group_recv), 13 * at, place, outs[name])

    loads = Loads(load_sem)
    loads.start("win0", win_h.at[0:3], win.at[0:3])
    loads.start("wout", wout_h, wout)
    loads.start("m1", m1_h, m1)
    loads.start("m2", m2_h, m2)

    def fetch(e):
        loads.start(("in", e), ein.at[e], g.at[2 * (e % 2)])
        loads.start(("out", e), eout.at[e], g.at[2 * (e % 2) + 1])

    loads.start("win1", win_h.at[3:6], win.at[3:6])
    fetch(0)
    fetch(1)
    rows_of = tokens.shape[0]

    def placement(i):
        row = lax.broadcasted_iota(jnp.int32, (PAD, rows_of), 0)
        column = lax.broadcasted_iota(jnp.int32, (PAD, rows_of), 1)
        hit = jnp.logical_and(row < SEQ, column == row + i * SEQ)
        return jnp.where(hit, 1.0, 0.0).astype(BF16)

    def padded(ref, i):
        return dot(placement(i), ref[...]).astype(BF16).reshape(2, HALF, D)

    def norm_rows(s, v):
        return (normalize(v)[0] * gain[s : s + 1] + bias[s : s + 1]).astype(BF16)

    def start_image(i):
        mo[i] = padded(tokens, i)
        for half in range(2):
            n0[i, half] = norm_rows(0, mo[i, half].astype(F32))
        streams[0, i] = mo[i, core].astype(F32)

    start_image(0)

    def rows(ref, i):
        return ref[i].reshape(PAD, D)

    def block(s, i):
        if s != 1:
            loads.need("win0", "wout", *(("win1",) if s else ()))
            return attention_forward(rows((n0, None, n2)[s], i), win, wout, s // 2, i, qkv, att, probs)
        loads.need("m1", "m2")
        hidden = dot(rows(n1, i), m1[...])
        dgelu[i] = hidden
        act[i] = (hidden * gelu_share(hidden)).astype(BF16)
        return dot(act[i], m2[...])

    normed = (n0, n1, n2, n3)

    def finish_forward(s, i):
        v = streams[s, i] + links.total(i, s % 2)
        streams[s + 1, i] = v
        normed[s + 1][i, core] = norm_rows(s + 1, v)
        links.gather((s, i), 2 * s + i, normed[s + 1].at[i])

    def hits():
        kept_choice = slots[...] < CAPACITY
        index = jnp.where(kept_choice, routes[...] * SLOTS + slots[...], -1)
        number = lax.broadcasted_iota(jnp.int32, (EXPERTS * SLOTS, rows_of), 0)
        return [number == index[k : k + 1] for k in range(2)]

    def make_pick():
        first, second = hits()
        flat = jnp.where(jnp.logical_or(first, second), 1.0, 0.0).astype(BF16)
        for i in range(2):
            pick[:, i * PAD : (i + 1) * PAD] = dot_nt(flat, placement(i)).astype(BF16)

    def make_spread():
        first, second = hits()
        flat = jnp.where(jnp.logical_or(first, second), 1.0, 0.0).astype(BF16)
        for i in range(2):
            spread[i * PAD : (i + 1) * PAD] = dot_nt(placement(i), flat).astype(BF16)

    def make_gate():
        gate[...] = sum(
            jnp.sum(jnp.where(hit, gates[k : k + 1], 0.0), axis=1, keepdims=True)
            for k, hit in enumerate(hits())
        )

    def make_cot():
        for i in range(2):
            cotp[i] = padded(cot, i)

    def make_drow():
        drow[...] = (dot(pick[...], cotp[...].reshape(2 * PAD, D)) * gate[...]).astype(BF16)

    fill = (lambda: start_image(1), make_pick, make_gate, make_cot, make_drow, make_spread)
    steps = [(s, i) for s in range(3) for i in range(2)]
    for at, (s, i) in enumerate(steps):
        if s > 0:
            links.arrived((s - 1, i))
        term = block(s, i)
        if at == 0:
            pl.semaphore_wait(barrier, 9)
        links.share(i, term)
        fill[at]()
        links.swap(i, s % 2)
        if at > 0:
            finish_forward(*steps[at - 1])
    finish_forward(*steps[-1])

    for i in range(2):
        links.arrived((2, i))
    buf[...] = dot(pick[...], n3[...].reshape(2 * PAD, D)).astype(BF16)
    for e in range(EXPERTS):
        cut = pl.ds(e * SLOTS, SLOTS)
        loads.need(("in", e), ("out", e))
        w_in = g[2 * (e % 2)].reshape(D, D)
        w_out = g[2 * (e % 2) + 1].reshape(D, D)
        a, slope = gelu_pair(dot(buf[cut], w_in))
        d = (slope * dot_nt(drow[cut], w_out)).astype(BF16)
        weighted[cut] = (dot(a, w_out) * gate[cut]).astype(BF16)
        dbuf[cut] = dot_nt(d, w_in).astype(BF16)
        weight_grad(ge, e, buf[cut], d)
        weight_grad(ge, EXPERTS + e, drow[cut], a)
        if e + 2 < EXPERTS:
            fetch(e + 2)
        if e == 1:
            groups["eay"].start(ge.at[0:2])
            groups["eaz"].start(ge.at[4:6])
        if e == 3:
            groups["eby"].start(ge.at[2:4])
            groups["ebz"].start(ge.at[6:8])
    for i in range(2):
        links.share(i, dot(spread[i * PAD : (i + 1) * PAD], dbuf[...]))
    for i in range(2):
        links.swap(i, 1)
    mo[...] = dot(spread[...], weighted[...]).astype(BF16).reshape(2, 2, HALF, D)
    for i in range(2):
        links.share_held(2 + i, mo.at[i])
    for i in range(2):
        dgelu[i] = gelu_slope(dgelu[i], gelu_share(dgelu[i]))

    def flat(ref):
        return ref[...].reshape(2 * PAD, D)

    def share(parity, i, value):
        links.share(i, value)
        links.swap(i, parity)

    def finish(s, parity, i, base, target, slot):
        dv, gain_term, bias_term = norm_back(streams[s, i], gain[s : s + 1], links.total(i, parity))
        sums[s : s + 1] = sums[s : s + 1] + gain_term
        sums[4 + s : 5 + s] = sums[4 + s : 5 + s] + bias_term
        v = base[i].astype(F32) + dv if s < 3 else base[i, core].astype(F32) + dv
        if s > 0:
            g2[i] = v
            target[i, core] = v.astype(BF16)
        else:
            target[i, core] = v
        links.gather((s, i), 2 * slot + i, target.at[i])

    def run(*names):
        for name in names:
            group, step = name.split(".")
            getattr(groups[group], step)()

    def heads_start(j, m, n, du):
        head_grad(g, m, flat(n), flat(du), stack)
        groups[f"a{j}y"].start(g.at[m : m + 1, :, :, :, 0:384])
        groups[f"a{j}z"].start(g.at[m : m + 1, :, :, :, 384:768])

    def dense_start():
        weight_grad(g, 0, flat(n1), dhid[0 : 2 * PAD])
        groups["m0"].start(g.at[0:1])
        weight_grad(g, 1, flat(du1), act[...].reshape(2 * PAD, D))
        groups["m1"].start(g.at[1:2])

    def output(i):
        out_o[i, core] = streams[3, i] + links.total(2 + i, 0)
        links.gather((4, i), 8 + i, out_o.at[i])

    def back(s, i):
        if s == 1:
            d = (dgelu[i] * dot_nt(rows(du1, i), m2[...])).astype(BF16)
            dhid[pl.ds(i * PAD, PAD)] = d
            return dot_nt(d, m1[...])
        du = du2 if s == 2 else du0
        return attention_backward(rows(du, i), win, wout, s // 2, i, qkv, att, probs, stack)

    def end(s, i):
        target = (token_o, du0, du1, du2)[s]
        finish(s, s % 2, i, cotp if s == 3 else g2, target, 3 - s)

    sums[...] = jnp.zeros_like(sums)
    run("eay.middle", "eaz.middle")
    end(3, 0)
    during = (
        lambda: links.swap(2, 0),
        lambda: run("eay.second"),
        lambda: links.swap(3, 0),
        lambda: run("ebz.second"),
        lambda: output(0),
        lambda: heads_start(0, 2, n0, du0),
    )
    after = (
        lambda: run("eby.middle", "ebz.middle"),
        lambda: (heads_start(1, 3, n2, du2), run("eaz.second")),
        lambda: run("eby.second", "a1y.middle", "a1z.middle"),
        lambda: (dense_start(), run("eay.relay", "eaz.relay")),
        lambda: run("a1y.second", "a1z.second", "eby.relay", "ebz.relay", "m0.middle", "m1.middle"),
        lambda: (run("eay.third", "eaz.third", "m0.second", "m1.second"), output(1)),
    )
    before = (3, 1)
    for at, (s, i) in enumerate((s, i) for s in (2, 1, 0) for i in range(2)):
        links.arrived((s + 1, i))
        links.share(i, back(s, i))
        during[at]()
        links.swap(i, s % 2)
        end(*before)
        before = (s, i)
        after[at]()
    end(*before)
    both = links.copy(sums, sums_in, 20, links.other)
    run("eby.third", "ebz.third")
    both.wait()
    wide = jnp.concatenate([sums[...] + sums_in[...], jnp.zeros((120, D), F32)], axis=0)
    gn[0] = wide.T.astype(BF16).reshape(4, 4, 48, 128)
    groups["n"].start(gn)
    run("a0y.second", "a0z.second", "a1y.third", "a1z.third", "n.second", "m0.third", "m1.third")
    run("a0y.third", "a0z.third", "n.third")
    run("eay.finish", "eaz.finish", "eby.finish", "ebz.finish", "a1y.finish", "a1z.finish")
    run("m0.finish", "m1.finish", "a0y.finish", "a0z.finish", "n.finish")
    for i in range(2):
        links.arrived((0, i))
        links.arrived((4, i))


def publish_kernel(*refs):
    count = (len(refs) - 3) // 2
    pads, sems = refs[-3:-1], refs[-1]
    targets = list(pads) + list(refs[count + 2 : 2 * count])
    copies = [pltpu.make_async_copy(refs[k], targets[k], sems.at[k]) for k in range(count)]
    for copy in copies:
        copy.start()
    for k in range(2):
        copies[k].wait()
        for i in range(2):
            refs[count + k][i * SEQ : (i + 1) * SEQ] = pads[k][i].reshape(PAD, D)[:SEQ]
    for copy in copies[2:]:
        copy.wait()


def link_scratch(channels, sems):
    return [
        pltpu.VMEM((2, HALF, D), F32),
        pltpu.VMEM((2, HALF, D), BF16),
        pltpu.VMEM((channels, HALF, D), BF16),
        pltpu.VMEM((channels, HALF, D), BF16),
        pltpu.VMEM((2 + channels, HALF, D), BF16),
        pltpu.SemaphoreType.DMA((sems,)),
        pltpu.SemaphoreType.DMA((sems,)),
    ]


def local(
    tokens,
    norm_gain,
    norm_bias,
    attn_in,
    attn_out,
    mlp_in,
    mlp_out,
    expert_in,
    expert_out,
    routes,
    slot_index,
    gate_weights,
    cotangent,
):
    head_width = attn_out.shape[1]
    slots = EXPERTS * SLOTS
    rows = tokens.shape[0]
    whole = pl.BlockSpec(memory_space=pltpu.VMEM)
    hbm = pl.BlockSpec(memory_space=pl.ANY)
    shape = jax.ShapeDtypeStruct
    half_rows = (2, 2, HALF, D)
    win = jnp.swapaxes(attn_in, 2, 3).reshape(6, head_width, D)
    scratch = (
        [pltpu.VMEM(half_rows, BF16)] * 7
        + [
            pltpu.VMEM((2, 3, 2, PAD, head_width), BF16),
            pltpu.VMEM((2, 2, PAD, head_width), BF16),
            pltpu.VMEM((2, 2, 3, PAD, PAD), BF16),
            pltpu.VMEM((2, PAD, D), BF16),
            pltpu.VMEM((2, PAD, D), F32),
            pltpu.VMEM((4, 2, HALF, D), F32),
            pltpu.VMEM((2, HALF, D), F32),
            pltpu.VMEM((slots, 2 * PAD), BF16),
            pltpu.VMEM((2 * PAD, slots), BF16),
            pltpu.VMEM((slots, 1), F32),
        ]
        + [pltpu.VMEM((slots, D), BF16)] * 4
        + [
            pltpu.VMEM((6, head_width, D), BF16),
            pltpu.VMEM((2, head_width, D), BF16),
            pltpu.VMEM((D, D), BF16),
            pltpu.VMEM((D, D), BF16),
            pltpu.VMEM((4, 4, 4, 48, D), BF16),
            pltpu.VMEM((2 * EXPERTS, 4, 4, 48, D), BF16),
            pltpu.VMEM((1, 4, 4, 48, 128), BF16),
            pltpu.VMEM((8, D), F32),
            pltpu.VMEM((8, D), F32),
        ]
        + link_scratch(4, 22)
        + [
            pltpu.SemaphoreType.DMA((13 * len(GROUPS),)),
            pltpu.SemaphoreType.DMA((13 * len(GROUPS),)),
            pltpu.SemaphoreType.DMA((13,)),
        ]
    )
    for spec in GROUPS.values():
        scratch += list(group_scratch(spec).values())
    results = pl.pallas_call(
        layers_kernel,
        out_shape=[
            shape(half_rows, F32),
            shape(half_rows, F32),
            shape((4, 24), F32),
            shape((4, 24), F32),
            shape((2, 3, 24, head_width), F32),
            shape((2, 24, head_width), F32),
            shape((24, D), F32),
            shape((24, D), F32),
            shape((EXPERTS, 24, D), F32),
            shape((EXPERTS, 24, D), F32),
        ],
        in_specs=[whole] * 7 + [hbm] * 6,
        out_specs=[whole] * 10,
        scratch_shapes=scratch,
        compiler_params=pltpu.CompilerParams(
            collective_id=1, has_side_effects=True, vmem_limit_bytes=63 << 20
        ),
        name="layers",
    )(
        tokens, cotangent, routes.T, slot_index.T, gate_weights.T, norm_gain, norm_bias, win, attn_out,
        mlp_in, mlp_out, expert_in.reshape(EXPERTS, 4, 4, 48, D), expert_out.reshape(EXPERTS, 4, 4, 48, D),
    )
    out, token_grad, gains, biases, heads_in, heads_out, m_in, m_out, e_in, e_out = pl.pallas_call(
        publish_kernel,
        out_shape=[shape((rows, D), F32)] * 2 + [shape(r.shape, r.dtype) for r in results[2:]],
        in_specs=[hbm] * len(results),
        out_specs=[whole] * len(results),
        scratch_shapes=[pltpu.VMEM(half_rows, F32)] * 2 + [pltpu.SemaphoreType.DMA((len(results),))],
        name="publish",
    )(*results)
    return (
        out,
        token_grad,
        gains,
        biases,
        heads_in,
        jnp.swapaxes(heads_out, 1, 2),
        m_in,
        m_out.T,
        e_in,
        jnp.swapaxes(e_out, 1, 2),
    )


def solution(mesh):
    placed = (
        P("dp", None),
        P(),
        P(),
        P(None, None, None, "tensor"),
        P(None, "tensor", None),
        P(None, "tensor"),
        P("tensor", None),
        P(None, None, "tensor"),
        P(None, "tensor", None),
        P("dp", None),
        P("dp", None),
        P("dp", None),
        P("dp", None),
    )
    return jax.shard_map(
        local,
        mesh=mesh,
        in_specs=placed,
        out_specs=(
            P("dp", None),
            P("dp", None),
            P(None, "dp"),
            P(None, "dp"),
            P(None, None, "dp", "tensor"),
            P(None, "tensor", "dp"),
            P("dp", "tensor"),
            P("tensor", "dp"),
            P(None, "dp", "tensor"),
            P(None, "tensor", "dp"),
        ),
        check_vma=False,
    )
```
